32 devices in a mesh: gx: 4 (over z), gy: 4 (over y, x), af: 2 (over core).
Axes of the slice: x: 2, y: 2, z: 4, core: 2. Of those that a mesh axis runs over, the one named last changes fastest.
Arguments:
- activations: bfloat16 [64, 8, 32, 128], P('af', 'gx', 'gy'), may hold values from -6 to 6
- filters: bfloat16 [3, 3, 3, 64, 64], P(None, None, None, 'af'), may hold values from -0.15625 to 0.15625
- conv_bias: float32 [64], P('af'), may hold values from -3 to 3
- grad_output: bfloat16 [64, 8, 32, 128], P('af', 'gx', 'gy'), may hold values from -23 to 23
Outputs:
- input_grads: bfloat16 [64, 8, 32, 128], P('af', 'gx', 'gy')
- filter_grads: float32 [3, 3, 3, 64, 64], P(None, None, None, 'af')
- bias_grads: float32 [64], P('af')
The draws below stay inside these ranges and needn't reach their ends.
All inputs are finite; a program needn't handle non-finite values.
Results may differ from the reference program's by a relative error of at most 0.0095.
Values may be sent and summed in bfloat16 or wider, within the bound.
A program may use at most 64 MiB of HBM per device.

```python
import math
import jax
import jax.numpy as jnp
from jax import lax

C_IN = 64
C_OUT = 64
NZ = 128
NX = 8
NY = 32


def draw_grad_output(key, part):
    along_x = jnp.arange(NX, dtype=jnp.float32) / max(NX - 1, 1)
    along_y = jnp.arange(NY, dtype=jnp.float32) / max(NY - 1, 1)
    sample = jnp.clip(jax.random.normal(key, (C_OUT, NX, NY, NZ), jnp.float32), -5.0, 5.0)
    ramp_up = (1.0 + 2.0 * along_x)[None, :, None, None] * (1.0 + 0.5 * along_y)[None, None, :, None]
    return (sample * ramp_up).astype(jnp.bfloat16)


def level_of(own_key, extent, shards, smallest, largest):
    loudness, own = 1.0, jax.random.fold_in(own_key, 6)
    for axis_at, shards_of in shards:
        draws = jnp.exp(jax.random.uniform(jax.random.fold_in(own, axis_at), (shards_of,), jnp.float32, smallest / len(shards), largest / len(shards)))
        loudness = loudness * jnp.repeat(draws, extent[axis_at] // shards_of).reshape([-1 if axis == axis_at else 1 for axis in range(len(extent))])
    return loudness


def scatter_about(own_key, shape, scale, bound, shards=(), kind=jnp.bfloat16):
    level = level_of(own_key, shape, shards, -0.22, 0.18) if shards else 1.0
    values = jax.random.normal(own_key, shape, jnp.float32) * scale * level
    return jnp.minimum(jnp.maximum(values, -bound), bound).astype(kind)


def setup_inputs(seed: int = 0) -> dict:
    streams_of = jax.random.split(jax.random.key(seed), 5)
    return {
        "activations": scatter_about(streams_of[0], (C_IN, NX, NY, NZ), 1.0, 6.0, ((0, 2), (1, 4), (2, 4))),
        "filters": scatter_about(streams_of[1], (3, 3, 3, C_OUT, C_IN), (27 * C_IN) ** -0.5, 0.15625, ((3, 2),)),
        "conv_bias": scatter_about(streams_of[2], (C_OUT,), 0.5, 3.0, ((0, 2),), jnp.float32),
        "grad_output": draw_grad_output(jax.random.fold_in(streams_of[4], 71), 0),
    }


def reference(activations, filters, conv_bias, grad_output):
    size_x, size_y, size_z = (activations.shape[1], activations.shape[2], activations.shape[3])
    acts_wide = activations.astype(jnp.float32)
    filt_wide = filters.astype(jnp.float32)
    padded = jnp.pad(acts_wide, ((0, 0), (1, 1), (1, 1), (1, 1)))
    pre_conv = jnp.zeros((filters.shape[3], size_x, size_y, size_z), jnp.float32) + conv_bias[:, None, None, None]
    for i in range(3):
        for j in range(3):
            for k in range(3):
                window = padded[:, i:i + size_x, j:j + size_y, k:k + size_z]
                pre_conv = pre_conv + jnp.einsum('oc,cxyz->oxyz', filt_wide[i, j, k], window)
    squash = jax.nn.sigmoid(pre_conv)
    gate_grad = (grad_output.astype(jnp.float32) * squash * (1.0 + pre_conv * (1.0 - squash))).astype(jnp.bfloat16)
    gate_wide = gate_grad.astype(jnp.float32)
    grad_padded = jnp.pad(gate_wide, ((0, 0), (1, 1), (1, 1), (1, 1)))
    running = jnp.zeros(activations.shape, jnp.float32)
    tap_terms = []
    for i in range(3):
        for j in range(3):
            for k in range(3):
                window = grad_padded[:, 2 - i:2 - i + size_x, 2 - j:2 - j + size_y, 2 - k:2 - k + size_z]
                running = running + jnp.einsum('oc,oxyz->cxyz', filt_wide[i, j, k], window)
                source = padded[:, i:i + size_x, j:j + size_y, k:k + size_z]
                tap_terms.append(jnp.einsum('oxyz,cxyz->oc', gate_wide, source))
    factor = 1.0 / math.sqrt(size_x * size_y * size_z)
    filter_grads = jnp.stack(tap_terms).reshape(filters.shape) * factor
    bias_grads = lax.optimization_barrier(jnp.sum(gate_wide, axis=(1, 2, 3))) * factor
    return (running.astype(jnp.bfloat16), filter_grads, bias_grads)
```

```python
import functools
import math

import jax
import jax.numpy as jnp
from jax import lax
from jax.experimental import pallas as pl
from jax.experimental.pallas import tpu as pltpu
from jax.sharding import PartitionSpec as P

MESH = pl.DeviceIdType.MESH
F32, BF16 = jnp.float32, jnp.bfloat16
SIDES = [(dx, dy) for dx in (-1, 0, 1) for dy in (-1, 0, 1) if (dx, dy) != (0, 0)]


def kernel(sizes, act_hbm, filt_hbm, bias_hbm, gout_hbm, igrad_ref, fgrad_ref,
           act_ref, filt_ref, bias_ref, gout_ref, load_sem, acts, gate, gout, gate_k, w_fwd, w_flip, w_bwd, part, part_in, pack, pack_in, mine, total,
           a_send, a_recv, h_send, h_recv, p_send, p_recv, g_send, g_recv, q_send, q_recv, r_sem, t_sem, near):
    n_gx, n_gy, px, py, nz, ch, rows, n_red, factor = sizes
    cin = 2 * ch
    inner = py * nz
    gx, gy, af = lax.axis_index("gx"), lax.axis_index("gy"), lax.axis_index("af")
    other = 1 - af
    group = n_gx * n_gy
    me = gx * n_gy + gy
    rounds = max(n_gx, n_gy) - 2

    loads = [pltpu.make_async_copy(src, dst, load_sem.at[at]) for at, (src, dst) in enumerate((
        (act_hbm, act_ref), (filt_hbm, filt_ref), (bias_hbm, bias_ref), (gout_hbm, gout_ref)))]
    for load in loads:
        load.start()

    def there(d):
        return (gx + d[0] >= 0) & (gx + d[0] < n_gx) & (gy + d[1] >= 0) & (gy + d[1] < n_gy)

    def back(d):
        return there((-d[0], -d[1]))

    barrier = pltpu.get_barrier_semaphore()
    around = sum(there(d).astype(jnp.int32) for d in SIDES)
    for d in SIDES:
        @pl.when(there(d))
        def _():
            for core in range(2):
                pl.semaphore_signal(
                    barrier, inc=1, device_id=(gx + d[0], gy + d[1], core), device_id_type=MESH)
    pl.semaphore_signal(barrier, inc=1, device_id=(gx, gy, other), device_id_type=MESH)

    def tell(at):
        for d in SIDES:
            @pl.when(there(d))
            def _():
                pl.semaphore_signal(
                    near.at[at], inc=1, device_id=(gx + d[0], gy + d[1], af), device_id_type=MESH)

    def hear(at):
        pl.semaphore_wait(near.at[at], around)

    def spans(d):
        dx, dy = d
        sx = {1: (px, 1), -1: (1, 1), 0: (1, px)}[dx]
        tx = {1: (0, 1), -1: (px + 1, 1), 0: (1, px)}[dx]
        sy = {1: (py, 1), -1: (1, 1), 0: (1, py)}[dy]
        ty = {1: (0, 1), -1: (py + 1, 1), 0: (1, py)}[dy]
        lanes = lambda s: pl.ds(s[0] * nz, s[1] * nz)
        return (pl.ds(*sx), lanes(sy)), (pl.ds(*tx), lanes(ty))

    for d in SIDES:
        tx, tl = spans(d)[1]
        missing = ~back(d)

        @pl.when(missing)
        def _():
            gate[tx, :, tl] = jnp.zeros((tx.size, ch, tl.size), BF16)

        if d[0] != 0 and d[1] != 0:
            missing &= (af == 1) | ~back((d[0], 0))

        @pl.when(missing)
        def _():
            acts[tx, :, :, tl] = jnp.zeros((tx.size, 2, ch, tl.size), BF16)

    loads[0].wait()
    for xo in range(px):
        acts[xo + 1, pl.ds(af, 1), :, nz:nz + inner] = (
            act_ref[:, xo].reshape(1, ch, inner))
    pl.semaphore_wait(barrier, 2 * around + 1)

    def act_copy(s, half, core):
        d = SIDES[s]
        (sx, sl), (tx, tl) = spans(d)
        return pltpu.make_async_remote_copy(
            src_ref=acts.at[sx, half, :, sl], dst_ref=acts.at[tx, half, :, tl],
            send_sem=a_send.at[2 * s + core], recv_sem=a_recv.at[2 * s + half],
            device_id=(gx + d[0], gy + d[1], core), device_id_type=MESH)

    def cores(s):
        return (1,) if SIDES[s][0] != 0 else (1, 0)

    def hand_on(at):
        plane = acts.at[pl.ds((0, px + 1)[at], 1)]
        return pltpu.make_async_remote_copy(
            src_ref=plane, dst_ref=plane, send_sem=h_send.at[at], recv_sem=h_recv.at[at],
            device_id=(gx, gy, 0), device_id_type=MESH)

    def gate_copy(s):
        d = SIDES[s]
        (sx, sl), (tx, tl) = spans(d)
        return pltpu.make_async_remote_copy(
            src_ref=gate.at[sx, :, sl], dst_ref=gate.at[tx, :, tl],
            send_sem=g_send.at[s], recv_sem=g_recv.at[s],
            device_id=(gx + d[0], gy + d[1], af), device_id_type=MESH)

    def partner_copy(which):
        block = acts.at[pl.ds(1, px), which, :, pl.ds(nz, inner)]
        return pltpu.make_async_remote_copy(
            src_ref=block, dst_ref=block, send_sem=p_send, recv_sem=p_recv,
            device_id=(gx, gy, other), device_id_type=MESH)

    order = sorted(range(8), key=lambda s: SIDES[s][1] != 0)
    for s in order:
        @pl.when(there(SIDES[s]))
        def _():
            for core in cores(s):
                act_copy(s, af, core).start()
    partner_copy(af).start()
    if rounds > 0:
        tell(0)

    for load in loads[1:]:
        load.wait()
    for xo in range(px):
        gout[xo] = gout_ref[:, xo].reshape(ch, inner)
    for i in range(3):
        for j in range(3):
            tap = filt_ref[i, j * 3 * ch:(j + 1) * 3 * ch, :]
            w_fwd[j, :, i * cin:(i + 1) * cin] = tap
            for k in range(3):
                w_flip[j, (2 - i) * ch:(3 - i) * ch, k * cin:(k + 1) * cin] = (
                    tap[k * ch:(k + 1) * ch, :])
    for j in range(3):
        w_bwd[j] = w_flip[j].astype(F32).T.astype(BF16)
    eye = (lax.broadcasted_iota(jnp.int32, (ch, ch), 0)
           == lax.broadcasted_iota(jnp.int32, (ch, ch), 1))
    bias = jnp.sum(jnp.where(eye, bias_ref[...], 0.0), axis=1, keepdims=True)

    for at in range(1, rounds):
        hear(at - 1)
        tell(at)

    for at, dx in enumerate((1, -1)):
        @pl.when((af == 1) & back((dx, 0)))
        def _():
            for s in order:
                if SIDES[s][0] == dx:
                    @pl.when(back(SIDES[s]))
                    def _():
                        for half in range(2):
                            act_copy(s, half, 1).wait_recv()
            hand_on(at).start()
    partner_copy(other).wait_recv()
    for s in order:
        if SIDES[s][0] == 0:
            @pl.when(back(SIDES[s]))
            def _():
                for half in range(2):
                    act_copy(s, half, 0).wait_recv()
    for at, dx in enumerate((1, -1)):
        @pl.when((af == 0) & back((dx, 0)))
        def _():
            hand_on(at).wait_recv()

    lane = lax.broadcasted_iota(jnp.int32, (1, nz), 1)

    def from_below(v):
        return jnp.where(lane == 0, 0.0, pltpu.roll(v, 1, 1))

    def from_above(v):
        return jnp.where(lane == nz - 1, 0.0, pltpu.roll(v, nz - 1, 1))

    step = 2 if py % 2 == 0 else 1
    bias_sum = jnp.zeros((ch, nz), F32)
    for xo in range(px):
        for y0 in range(0, py, step):
            acc = None
            for j in range(3):
                window = acts[xo:xo + 3, :, :, (y0 + j) * nz:(y0 + j + step) * nz]
                term = jnp.dot(w_fwd[j], window.reshape(3 * cin, step * nz),
                               preferred_element_type=F32)
                acc = term if acc is None else acc + term
            for u in range(step):
                cut = acc[:, u * nz:(u + 1) * nz]
                pre = (cut[ch:2 * ch] + from_below(cut[:ch]) + from_above(cut[2 * ch:])) + bias
                lanes = slice((y0 + u) * nz, (y0 + u + 1) * nz)
                squash = 1.0 / (1.0 + jnp.exp(-pre))
                g = gout[xo, :, lanes].astype(F32) * squash * (1.0 + pre * (1.0 - squash))
                rounded = g.astype(BF16)
                g = rounded.astype(F32)
                bias_sum = bias_sum + g
                gate[xo + 1, :, (y0 + u + 1) * nz:(y0 + u + 2) * nz] = rounded
                gate_k[xo, 0:ch, lanes] = from_above(g).astype(BF16)
                gate_k[xo, ch:2 * ch, lanes] = rounded
                gate_k[xo, 2 * ch:3 * ch, lanes] = from_below(g).astype(BF16)

    head = ch
    main, fold = 3 * ch, 3 * ch // 2
    whole = jnp.sum(bias_sum, axis=1, keepdims=True) * factor + jnp.zeros((ch, 2 * cin), F32)
    wide = lax.broadcasted_iota(jnp.int32, (1, 2 * cin), 1)

    def two_parts(v):
        high = v.astype(BF16).astype(F32)
        return jnp.where(wide < cin, high, v - high)

    pack[0:head, :] = two_parts(whole).astype(BF16)
    used = head + 3 * (main + fold)
    if n_red * rows > used:
        pack[used:n_red * rows, :] = jnp.zeros((n_red * rows - used, 2 * cin), BF16)

    def scatter(first, count):
        for b in range(first, first + count):
            chip = 2 * b + af
            own = (af == 1) & (chip == me)
            block = pack.at[pl.ds(b * rows, rows)]
            slot = pack_in.at[pl.ds(pl.multiple_of(me * rows, 16), rows)]

            @pl.when(own)
            def _():
                pltpu.make_async_copy(block, slot, r_sem.at[1]).start()

            @pl.when(~own)
            def _():
                pltpu.make_async_remote_copy(
                    src_ref=block, dst_ref=slot, send_sem=r_sem.at[0], recv_sem=r_sem.at[1],
                    device_id=(chip // n_gy, lax.rem(chip, n_gy), 1), device_id_type=MESH).start()

    ready = 0
    for j in range(3):
        acc = None
        for xo in range(px):
            window = acts[xo:xo + 3, :, :, j * nz:j * nz + inner].reshape(3 * cin, inner)
            term = lax.dot_general(gate_k[xo], window, (((1,), (1,)), ((), ())),
                                   preferred_element_type=F32)
            acc = term if acc is None else acc + term
        acc = (acc * factor).astype(BF16)
        base = head + j * (main + fold)
        pack[base:base + main, :] = acc[:, :2 * cin]
        pack[base + main:base + main + fold, 0:cin] = acc[:fold, 2 * cin:]
        pack[base + main:base + main + fold, cin:2 * cin] = acc[fold:, 2 * cin:]
        done = n_red if j == 2 else (base + main + fold) // rows
        if j == 0 and rounds > 0:
            hear(rounds - 1)
        if done > ready:
            scatter(ready, done - ready)
        ready = done

    for s in order:
        @pl.when(there(SIDES[s]))
        def _():
            gate_copy(s).start()

    def settle(ref, count, sem):
        block = ref.at[pl.ds(0, count * rows)]
        return pltpu.make_async_copy(block, block, sem)

    half, at_block = lax.rem(me, 2), me // 2
    reducer = (af == 1) & (me < 2 * n_red)
    here = pl.multiple_of(at_block * rows, 16)

    def share(peer):
        own = (half == 1) & (peer == me)
        place = total.at[pl.ds(here, rows)]

        @pl.when(own)
        def _():
            pltpu.make_async_copy(mine, place, t_sem.at[1]).start()

        @pl.when(~own)
        def _():
            pltpu.make_async_remote_copy(
                src_ref=mine, dst_ref=place, send_sem=t_sem.at[0], recv_sem=t_sem.at[1],
                device_id=(peer // n_gy, peer % n_gy, half), device_id_type=MESH).start()

    @pl.when(reducer)
    def _():
        settle(pack_in, group, r_sem.at[1]).wait()

        def add(t, v):
            return v + pack_in[pl.ds(pl.multiple_of(t * rows, 16), rows), :].astype(F32)

        summed = pack_in[0:rows, :].astype(F32)
        if group <= 32:
            for t in range(1, group):
                summed = add(t, summed)
        else:
            summed = lax.fori_loop(1, group, add, summed)
        both = two_parts(summed + pltpu.roll(summed, cin, 1))
        at = here + lax.broadcasted_iota(jnp.int32, (rows, 1), 0)
        mine[...] = jnp.where(at < head, both, summed).astype(BF16)
        if group <= 32:
            for peer in range(group):
                share(peer)
        else:
            lax.fori_loop(0, group, lambda peer, _: share(peer) or 0, 0)

    for s in order:
        @pl.when(back(SIDES[s]))
        def _():
            gate_copy(s).wait_recv()

    def part_copy(xo):
        return pltpu.make_async_remote_copy(
            src_ref=part.at[xo, other], dst_ref=part_in.at[xo],
            send_sem=q_send.at[xo], recv_sem=q_recv.at[xo],
            device_id=(gx, gy, other), device_id_type=MESH)

    for xo in range(px):
        for y0 in range(0, py, step):
            acc = None
            for j in range(3):
                at = y0 + 2 - j
                window = gate[xo:xo + 3, :, at * nz:(at + step) * nz].reshape(3 * ch, step * nz)
                term = jnp.dot(w_bwd[j], window, preferred_element_type=F32)
                acc = term if acc is None else acc + term
            for u in range(step):
                cut = acc[:, u * nz:(u + 1) * nz]
                full = (cut[cin:2 * cin] + from_above(cut[:cin]) + from_below(cut[2 * cin:]))
                part[xo, :, :, (y0 + u) * nz:(y0 + u + 1) * nz] = full.reshape(2, ch, nz)
        part_copy(xo).start()

    for xo in range(px):
        part_copy(xo).wait_recv()
        mine = part[xo, pl.ds(af, 1), :, :].reshape(ch, inner)
        igrad_ref[:, xo] = (mine + part_in[xo]).reshape(ch, py, nz).astype(BF16)

    for s in order:
        @pl.when(there(SIDES[s]))
        def _():
            for core in cores(s):
                act_copy(s, af, core).wait_send()
            gate_copy(s).wait_send()
    for at, dx in enumerate((1, -1)):
        @pl.when((af == 1) & back((dx, 0)))
        def _():
            hand_on(at).wait_send()
    partner_copy(af).wait_send()
    for xo in range(px):
        part_copy(xo).wait_send()

    kept = reducer & (half == 1)

    @pl.when(kept)
    def _():
        settle(pack, n_red - 1, r_sem.at[0]).wait()
        settle(pack_in, group - 1, t_sem.at[0]).wait()

    @pl.when(~kept)
    def _():
        settle(pack, n_red, r_sem.at[0]).wait()

    @pl.when(reducer & (half == 0))
    def _():
        settle(pack_in, group, t_sem.at[0]).wait()

    settle(total, n_red, t_sem.at[1]).wait()
    fgrad_ref[...] = total[...]


def unpack(sizes, igrad_ref, packed, igrad_out, fgrad_out, bias_out, taps, bias, sems):
    ch, cin = sizes
    early = pltpu.make_async_copy(igrad_ref, igrad_out, sems.at[0])
    early.start()
    head, main, fold = ch, 3 * ch, 3 * ch // 2
    column = (packed[0:head, :].astype(F32) + pltpu.roll(packed[0:head, :].astype(F32), cin, 1))[:, :1]
    eye = (lax.broadcasted_iota(jnp.int32, (ch, ch), 0)
           == lax.broadcasted_iota(jnp.int32, (ch, ch), 1))
    bias[...] = jnp.sum(jnp.where(eye, column, 0.0), axis=0, keepdims=True)
    small = pltpu.make_async_copy(bias, bias_out, sems.at[1])
    small.start()
    for j in range(3):
        base = head + j * (main + fold)
        block = packed[base:base + main + fold, :].astype(F32)
        at = j * main
        taps[0, at:at + main, :] = block[:main, :cin]
        taps[1, at:at + main, :] = block[:main, cin:]
        taps[2, at:at + fold, :] = block[main:, :cin]
        taps[2, at + fold:at + main, :] = block[main:, cin:]
    large = pltpu.make_async_copy(taps, fgrad_out, sems.at[2])
    large.start()
    early.wait()
    small.wait()
    large.wait()


def per_device(activations, filters, conv_bias, grad_output):
    ch, px, py, nz = activations.shape
    n_gx, n_gy = lax.axis_size("gx"), lax.axis_size("gy")
    group = n_gx * n_gy
    cin = 2 * ch
    inner = py * nz
    factor = 1.0 / math.sqrt(px * n_gx * py * n_gy * nz)
    used = ch + 3 * (3 * ch + 3 * ch // 2)
    rows = 16 * (-(-(used // 16) // (group // 2)))
    n_red = -(-used // rows)

    vmem = pl.BlockSpec(memory_space=pltpu.VMEM)
    hbm = pl.BlockSpec(memory_space=pltpu.HBM)
    dma = pltpu.SemaphoreType.DMA
    igrad, packed = pl.pallas_call(
        functools.partial(kernel, (n_gx, n_gy, px, py, nz, ch, rows, n_red, factor)),
        out_shape=(jax.ShapeDtypeStruct((ch, px, py, nz), BF16),
                   jax.ShapeDtypeStruct((n_red * rows, 2 * cin), BF16)),
        in_specs=[hbm] * 4,
        out_specs=(vmem, vmem),
        scratch_shapes=[
            pltpu.VMEM((ch, px, py, nz), BF16),
            pltpu.VMEM((3, 9 * ch, cin), BF16),
            pltpu.VMEM((1, ch), F32),
            pltpu.VMEM((ch, px, py, nz), BF16),
            dma((4,)),
            pltpu.VMEM((px + 2, 2, ch, (py + 2) * nz), BF16),
            pltpu.VMEM((px + 2, ch, (py + 2) * nz), BF16),
            pltpu.VMEM((px, ch, inner), BF16),
            pltpu.VMEM((px, 3 * ch, inner), BF16),
            pltpu.VMEM((3, 3 * ch, 3 * cin), BF16),
            pltpu.VMEM((3, 3 * ch, 3 * cin), BF16),
            pltpu.VMEM((3, 3 * cin, 3 * ch), BF16),
            pltpu.VMEM((px, 2, ch, inner), F32),
            pltpu.VMEM((px, ch, inner), F32),
            pltpu.VMEM((n_red * rows, 2 * cin), BF16),
            pltpu.VMEM((group * rows, 2 * cin), BF16),
            pltpu.VMEM((rows, 2 * cin), BF16),
            pltpu.VMEM((n_red * rows, 2 * cin), BF16),
            dma((16,)), dma((16,)), dma((2,)), dma((2,)), dma, dma, dma((8,)), dma((8,)),
            dma((px,)), dma((px,)), dma((2,)), dma((2,)),
            pltpu.SemaphoreType.REGULAR((max(1, max(n_gx, n_gy) - 2),)),
        ],
        compiler_params=pltpu.CompilerParams(
            collective_id=0, has_side_effects=True, vmem_limit_bytes=24 * 1024 * 1024),
    )(*[pltpu.with_memory_space_constraint(v, pltpu.HBM) for v in (activations, filters.reshape(3, 9 * ch, cin), conv_bias.reshape(1, ch), grad_output)])
    input_grads, filter_grads, bias_grads = pl.pallas_call(
        functools.partial(unpack, (ch, cin)),
        out_shape=(jax.ShapeDtypeStruct(activations.shape, BF16),
                   jax.ShapeDtypeStruct((3, 9 * ch, cin), F32),
                   jax.ShapeDtypeStruct((1, ch), F32)),
        in_specs=[vmem] * 2,
        out_specs=(hbm,) * 3,
        scratch_shapes=[pltpu.VMEM((3, 9 * ch, cin), F32), pltpu.VMEM((1, ch), F32), dma((3,))],
        compiler_params=pltpu.CompilerParams(vmem_limit_bytes=8 * 1024 * 1024),
    )(igrad, packed)
    return (input_grads, filter_grads.reshape(filters.shape), bias_grads.reshape(ch))


def solution(mesh):
    return jax.shard_map(
        per_device,
        mesh=mesh,
        in_specs=(
            P("af", "gx", "gy", None),
            P(None, None, None, "af", None),
            P("af"),
            P("af", "gx", "gy", None),
        ),
        out_specs=(P("af", "gx", "gy", None), P(None, None, None, "af", None), P("af")),
        check_vma=False,
    )
```

```python
import functools
import math

import jax
import jax.numpy as jnp
from jax import lax
from jax.experimental import pallas as pl
from jax.experimental.pallas import tpu as pltpu
from jax.sharding import PartitionSpec as P

MESH = pl.DeviceIdType.MESH
F32, BF16 = jnp.float32, jnp.bfloat16
SIDES = [(dx, dy) for dx in (-1, 0, 1) for dy in (-1, 0, 1) if (dx, dy) != (0, 0)]


def kernel(sizes, act_hbm, filt_hbm, bias_hbm, gout_hbm, igrad_ref, fgrad_ref,
           act_ref, filt_ref, bias_ref, gout_ref, load_sem, acts, gate, gout, gate_k, w_fwd, w_flip, w_bwd, part, part_in, pack, pack_in, mine, total,
           a_send, a_recv, h_send, h_recv, p_send, p_recv, g_send, g_recv, q_send, q_recv, r_sem, t_sem, near):
    n_gx, n_gy, px, py, nz, ch, rows, n_red, factor = sizes
    cin = 2 * ch
    inner = py * nz
    gx, gy, af = lax.axis_index("gx"), lax.axis_index("gy"), lax.axis_index("af")
    other = 1 - af
    group = n_gx * n_gy
    me = gx * n_gy + gy
    rounds = max(n_gx, n_gy) - 2

    loads = [pltpu.make_async_copy(src, dst, load_sem.at[at]) for at, (src, dst) in enumerate((
        (act_hbm, act_ref), (filt_hbm, filt_ref), (bias_hbm, bias_ref), (gout_hbm, gout_ref)))]
    for load in loads:
        load.start()

    def there(d):
        return (gx + d[0] >= 0) & (gx + d[0] < n_gx) & (gy + d[1] >= 0) & (gy + d[1] < n_gy)

    def back(d):
        return there((-d[0], -d[1]))

    barrier = pltpu.get_barrier_semaphore()
    around = sum(there(d).astype(jnp.int32) for d in SIDES)
    for d in SIDES:
        @pl.when(there(d))
        def _():
            for core in range(2):
                pl.semaphore_signal(
                    barrier, inc=1, device_id=(gx + d[0], gy + d[1], core), device_id_type=MESH)
    pl.semaphore_signal(barrier, inc=1, device_id=(gx, gy, other), device_id_type=MESH)

    def tell(at):
        for d in SIDES:
            @pl.when(there(d))
            def _():
                pl.semaphore_signal(
                    near.at[at], inc=1, device_id=(gx + d[0], gy + d[1], af), device_id_type=MESH)

    def hear(at):
        pl.semaphore_wait(near.at[at], around)

    def spans(d):
        dx, dy = d
        sx = {1: (px, 1), -1: (1, 1), 0: (1, px)}[dx]
        tx = {1: (0, 1), -1: (px + 1, 1), 0: (1, px)}[dx]
        sy = {1: (py, 1), -1: (1, 1), 0: (1, py)}[dy]
        ty = {1: (0, 1), -1: (py + 1, 1), 0: (1, py)}[dy]
        lanes = lambda s: pl.ds(s[0] * nz, s[1] * nz)
        return (pl.ds(*sx), lanes(sy)), (pl.ds(*tx), lanes(ty))

    for d in SIDES:
        tx, tl = spans(d)[1]
        missing = ~back(d)

        @pl.when(missing)
        def _():
            gate[tx, :, tl] = jnp.zeros((tx.size, ch, tl.size), BF16)

        if d[0] != 0 and d[1] != 0:
            missing &= (af == 1) | ~back((d[0], 0))

        @pl.when(missing)
        def _():
            acts[tx, :, :, tl] = jnp.zeros((tx.size, 2, ch, tl.size), BF16)

    loads[0].wait()
    for xo in range(px):
        acts[xo + 1, pl.ds(af, 1), :, nz:nz + inner] = (
            act_ref[:, xo].reshape(1, ch, inner))
    pl.semaphore_wait(barrier, 2 * around + 1)

    def act_copy(s, half, core):
        d = SIDES[s]
        (sx, sl), (tx, tl) = spans(d)
        return pltpu.make_async_remote_copy(
            src_ref=acts.at[sx, half, :, sl], dst_ref=acts.at[tx, half, :, tl],
            send_sem=a_send.at[2 * s + core], recv_sem=a_recv.at[2 * s + half],
            device_id=(gx + d[0], gy + d[1], core), device_id_type=MESH)

    def cores(s):
        return (1,) if SIDES[s][0] != 0 else (1, 0)

    def hand_on(at, half):
        plane = acts.at[pl.ds((0, px + 1)[at], 1), half]
        return pltpu.make_async_remote_copy(
            src_ref=plane, dst_ref=plane, send_sem=h_send.at[2 * at + half], recv_sem=h_recv.at[2 * at + half],
            device_id=(gx, gy, 0), device_id_type=MESH)

    def gate_copy(s):
        d = SIDES[s]
        (sx, sl), (tx, tl) = spans(d)
        return pltpu.make_async_remote_copy(
            src_ref=gate.at[sx, :, sl], dst_ref=gate.at[tx, :, tl],
            send_sem=g_send.at[s], recv_sem=g_recv.at[s],
            device_id=(gx + d[0], gy + d[1], af), device_id_type=MESH)

    def partner_copy(which):
        block = acts.at[pl.ds(1, px), which, :, pl.ds(nz, inner)]
        return pltpu.make_async_remote_copy(
            src_ref=block, dst_ref=block, send_sem=p_send, recv_sem=p_recv,
            device_id=(gx, gy, other), device_id_type=MESH)

    order = sorted(range(8), key=lambda s: (SIDES[s][0] == 0) * 2 + (SIDES[s][1] == 0))
    for s in order:
        @pl.when(there(SIDES[s]))
        def _():
            for core in cores(s):
                act_copy(s, af, core).start()
    partner_copy(af).start()
    if rounds > 0:
        tell(0)

    for load in loads[1:]:
        load.wait()
    for xo in range(px):
        gout[xo] = gout_ref[:, xo].reshape(ch, inner)
    for i in range(3):
        for j in range(3):
            w_fwd[j, :, i * cin:(i + 1) * cin] = filt_ref[i, j * 3 * ch:(j + 1) * 3 * ch, :]
    eye = (lax.broadcasted_iota(jnp.int32, (ch, ch), 0)
           == lax.broadcasted_iota(jnp.int32, (ch, ch), 1))
    bias = jnp.sum(jnp.where(eye, bias_ref[...], 0.0), axis=1, keepdims=True)

    for at in range(1, rounds):
        hear(at - 1)
        tell(at)

    for half in (1, 0):
        for at, dx in enumerate((1, -1)):
            @pl.when((af == 1) & back((dx, 0)))
            def _():
                for s in order:
                    if SIDES[s][0] == dx:
                        @pl.when(back(SIDES[s]))
                        def _():
                            act_copy(s, half, 1).wait_recv()
                hand_on(at, half).start()
    partner_copy(other).wait_recv()
    for s in order:
        if SIDES[s][0] == 0:
            @pl.when(back(SIDES[s]))
            def _():
                for half in range(2):
                    act_copy(s, half, 0).wait_recv()
    for at, dx in enumerate((1, -1)):
        @pl.when((af == 0) & back((dx, 0)))
        def _():
            for half in range(2):
                hand_on(at, half).wait_recv()

    lane = lax.broadcasted_iota(jnp.int32, (1, nz), 1)

    def from_below(v):
        return jnp.where(lane == 0, 0.0, pltpu.roll(v, 1, 1))

    def from_above(v):
        return jnp.where(lane == nz - 1, 0.0, pltpu.roll(v, nz - 1, 1))

    step = 2 if py % 2 == 0 else 1
    bias_sum = jnp.zeros((ch, nz), F32)
    for xo in range(px):
        for y0 in range(0, py, step):
            acc = None
            for j in range(3):
                window = acts[xo:xo + 3, :, :, (y0 + j) * nz:(y0 + j + step) * nz]
                term = jnp.dot(w_fwd[j], window.reshape(3 * cin, step * nz),
                               preferred_element_type=F32)
                acc = term if acc is None else acc + term
            for u in range(step):
                cut = acc[:, u * nz:(u + 1) * nz]
                pre = (cut[ch:2 * ch] + from_below(cut[:ch]) + from_above(cut[2 * ch:])) + bias
                lanes = slice((y0 + u) * nz, (y0 + u + 1) * nz)
                squash = 1.0 / (1.0 + jnp.exp(-pre))
                g = gout[xo, :, lanes].astype(F32) * squash * (1.0 + pre * (1.0 - squash))
                rounded = g.astype(BF16)
                g = rounded.astype(F32)
                bias_sum = bias_sum + g
                gate[xo + 1, :, (y0 + u + 1) * nz:(y0 + u + 2) * nz] = rounded
                gate_k[xo, 0:ch, lanes] = from_above(g).astype(BF16)
                gate_k[xo, ch:2 * ch, lanes] = rounded
                gate_k[xo, 2 * ch:3 * ch, lanes] = from_below(g).astype(BF16)

    head = ch
    main, fold = 3 * ch, 3 * ch // 2
    whole = jnp.sum(bias_sum, axis=1, keepdims=True) * factor + jnp.zeros((ch, 2 * cin), F32)
    wide = lax.broadcasted_iota(jnp.int32, (1, 2 * cin), 1)

    def two_parts(v):
        high = v.astype(BF16).astype(F32)
        return jnp.where(wide < cin, high, v - high)

    pack[0:head, :] = two_parts(whole).astype(BF16)
    used = head + 3 * (main + fold)
    if n_red * rows > used:
        pack[used:n_red * rows, :] = jnp.zeros((n_red * rows - used, 2 * cin), BF16)

    def way(chip):
        at = chip // n_gy
        return max(at, n_gx - 1 - at) + at

    homes = sorted(range(0, group - 1, 2), key=lambda chip: (way(chip), -chip))[:n_red]
    homes.sort(key=lambda chip: (-way(chip), chip))

    def scatter(first, count):
        for b in range(first, first + count):
            chip = homes[b] + af
            own = (af == 1) & (chip == me)
            block = pack.at[pl.ds(b * rows, rows)]
            slot = pack_in.at[pl.ds(pl.multiple_of(me * rows, 16), rows)]

            @pl.when(own)
            def _():
                pltpu.make_async_copy(block, slot, r_sem.at[1]).start()

            @pl.when(~own)
            def _():
                pltpu.make_async_remote_copy(
                    src_ref=block, dst_ref=slot, send_sem=r_sem.at[0], recv_sem=r_sem.at[1],
                    device_id=(chip // n_gy, lax.rem(chip, n_gy), 1), device_id_type=MESH).start()

    ready = 0
    for j in range(3):
        acc = None
        for xo in range(px):
            window = acts[xo:xo + 3, :, :, j * nz:j * nz + inner].reshape(3 * cin, inner)
            term = lax.dot_general(gate_k[xo], window, (((1,), (1,)), ((), ())),
                                   preferred_element_type=F32)
            acc = term if acc is None else acc + term
        acc = (acc * factor).astype(BF16)
        base = head + j * (main + fold)
        pack[base:base + main, :] = acc[:, :2 * cin]
        pack[base + main:base + main + fold, 0:cin] = acc[:fold, 2 * cin:]
        pack[base + main:base + main + fold, cin:2 * cin] = acc[fold:, 2 * cin:]
        done = n_red if j == 2 else (base + main + fold) // rows
        if j == 0 and rounds > 0:
            hear(rounds - 1)
        if done > ready:
            scatter(ready, done - ready)
        ready = done

    for s in order:
        @pl.when(there(SIDES[s]))
        def _():
            gate_copy(s).start()

    for i in range(3):
        for j in range(3):
            for k in range(3):
                at = (3 * j + k) * ch
                w_flip[j, (2 - i) * ch:(3 - i) * ch, k * cin:(k + 1) * cin] = filt_ref[i, at:at + ch, :]
    for j in range(3):
        w_bwd[j] = w_flip[j].astype(F32).T.astype(BF16)

    def settle(ref, count, sem):
        block = ref.at[pl.ds(0, count * rows)]
        return pltpu.make_async_copy(block, block, sem)

    half = lax.rem(me, 2)
    at_block, found = jnp.int32(0), jnp.int32(0)
    for b in range(n_red):
        here = (me - half == homes[b]).astype(jnp.int32)
        at_block, found = at_block + b * here, found + here
    reducer = (af == 1) & (found > 0)
    here = pl.multiple_of(at_block * rows, 16)

    def share(peer):
        own = (half == 1) & (peer == me)
        place = total.at[pl.ds(here, rows)]

        @pl.when(own)
        def _():
            pltpu.make_async_copy(mine, place, t_sem.at[1]).start()

        @pl.when(~own)
        def _():
            pltpu.make_async_remote_copy(
                src_ref=mine, dst_ref=place, send_sem=t_sem.at[0], recv_sem=t_sem.at[1],
                device_id=(peer // n_gy, peer % n_gy, half), device_id_type=MESH).start()

    @pl.when(reducer)
    def _():
        settle(pack_in, group, r_sem.at[1]).wait()

        def add(t, v):
            return v + pack_in[pl.ds(pl.multiple_of(t * rows, 16), rows), :].astype(F32)

        summed = pack_in[0:rows, :].astype(F32)
        if group <= 32:
            for t in range(1, group):
                summed = add(t, summed)
        else:
            summed = lax.fori_loop(1, group, add, summed)
        both = two_parts(summed + pltpu.roll(summed, cin, 1))
        at = here + lax.broadcasted_iota(jnp.int32, (rows, 1), 0)
        mine[...] = jnp.where(at < head, both, summed).astype(BF16)
        if group <= 32:
            for peer in range(group):
                share(peer)
        else:
            lax.fori_loop(0, group, lambda peer, _: share(peer) or 0, 0)

    for s in order:
        @pl.when(back(SIDES[s]))
        def _():
            gate_copy(s).wait_recv()

    def part_copy(xo):
        return pltpu.make_async_remote_copy(
            src_ref=part.at[xo, other], dst_ref=part_in.at[xo],
            send_sem=q_send.at[xo], recv_sem=q_recv.at[xo],
            device_id=(gx, gy, other), device_id_type=MESH)

    for xo in range(px):
        for y0 in range(0, py, step):
            acc = None
            for j in range(3):
                at = y0 + 2 - j
                window = gate[xo:xo + 3, :, at * nz:(at + step) * nz].reshape(3 * ch, step * nz)
                term = jnp.dot(w_bwd[j], window, preferred_element_type=F32)
                acc = term if acc is None else acc + term
            for u in range(step):
                cut = acc[:, u * nz:(u + 1) * nz]
                full = (cut[cin:2 * cin] + from_above(cut[:cin]) + from_below(cut[2 * cin:]))
                part[xo, :, :, (y0 + u) * nz:(y0 + u + 1) * nz] = full.reshape(2, ch, nz)
        part_copy(xo).start()

    for xo in range(px):
        part_copy(xo).wait_recv()
        mine = part[xo, pl.ds(af, 1), :, :].reshape(ch, inner)
        igrad_ref[:, xo] = (mine + part_in[xo]).reshape(ch, py, nz).astype(BF16)

    for s in order:
        @pl.when(there(SIDES[s]))
        def _():
            for core in cores(s):
                act_copy(s, af, core).wait_send()
            gate_copy(s).wait_send()
    for at, dx in enumerate((1, -1)):
        @pl.when((af == 1) & back((dx, 0)))
        def _():
            for half in range(2):
                hand_on(at, half).wait_send()
    partner_copy(af).wait_send()
    for xo in range(px):
        part_copy(xo).wait_send()

    kept = reducer & (half == 1)

    @pl.when(kept)
    def _():
        settle(pack, n_red - 1, r_sem.at[0]).wait()
        settle(pack_in, group - 1, t_sem.at[0]).wait()

    @pl.when(~kept)
    def _():
        settle(pack, n_red, r_sem.at[0]).wait()

    @pl.when(reducer & (half == 0))
    def _():
        settle(pack_in, group, t_sem.at[0]).wait()

    settle(total, n_red, t_sem.at[1]).wait()
    fgrad_ref[...] = total[...]


def unpack(sizes, igrad_ref, packed, igrad_out, fgrad_out, bias_out, taps, bias, sems):
    ch, cin = sizes
    early = pltpu.make_async_copy(igrad_ref, igrad_out, sems.at[0])
    early.start()
    head, main, fold = ch, 3 * ch, 3 * ch // 2
    column = (packed[0:head, :].astype(F32) + pltpu.roll(packed[0:head, :].astype(F32), cin, 1))[:, :1]
    eye = (lax.broadcasted_iota(jnp.int32, (ch, ch), 0)
           == lax.broadcasted_iota(jnp.int32, (ch, ch), 1))
    bias[...] = jnp.sum(jnp.where(eye, column, 0.0), axis=0, keepdims=True)
    small = pltpu.make_async_copy(bias, bias_out, sems.at[1])
    small.start()
    for j in range(3):
        base = head + j * (main + fold)
        block = packed[base:base + main + fold, :].astype(F32)
        at = j * main
        taps[0, at:at + main, :] = block[:main, :cin]
        taps[1, at:at + main, :] = block[:main, cin:]
        taps[2, at:at + fold, :] = block[main:, :cin]
        taps[2, at + fold:at + main, :] = block[main:, cin:]
    large = pltpu.make_async_copy(taps, fgrad_out, sems.at[2])
    large.start()
    early.wait()
    small.wait()
    large.wait()


def per_device(activations, filters, conv_bias, grad_output):
    ch, px, py, nz = activations.shape
    n_gx, n_gy = lax.axis_size("gx"), lax.axis_size("gy")
    group = n_gx * n_gy
    cin = 2 * ch
    inner = py * nz
    factor = 1.0 / math.sqrt(px * n_gx * py * n_gy * nz)
    used = ch + 3 * (3 * ch + 3 * ch // 2)
    rows = 16 * (-(-(used // 16) // (group // 2 * 3 // 4)))
    n_red = -(-used // rows)

    vmem = pl.BlockSpec(memory_space=pltpu.VMEM)
    hbm = pl.BlockSpec(memory_space=pltpu.HBM)
    dma = pltpu.SemaphoreType.DMA
    igrad, packed = pl.pallas_call(
        functools.partial(kernel, (n_gx, n_gy, px, py, nz, ch, rows, n_red, factor)),
        out_shape=(jax.ShapeDtypeStruct((ch, px, py, nz), BF16),
                   jax.ShapeDtypeStruct((n_red * rows, 2 * cin), BF16)),
        in_specs=[hbm] * 4,
        out_specs=(vmem, vmem),
        scratch_shapes=[
            pltpu.VMEM((ch, px, py, nz), BF16),
            pltpu.VMEM((3, 9 * ch, cin), BF16),
            pltpu.VMEM((1, ch), F32),
            pltpu.VMEM((ch, px, py, nz), BF16),
            dma((4,)),
            pltpu.VMEM((px + 2, 2, ch, (py + 2) * nz), BF16),
            pltpu.VMEM((px + 2, ch, (py + 2) * nz), BF16),
            pltpu.VMEM((px, ch, inner), BF16),
            pltpu.VMEM((px, 3 * ch, inner), BF16),
            pltpu.VMEM((3, 3 * ch, 3 * cin), BF16),
            pltpu.VMEM((3, 3 * ch, 3 * cin), BF16),
            pltpu.VMEM((3, 3 * cin, 3 * ch), BF16),
            pltpu.VMEM((px, 2, ch, inner), F32),
            pltpu.VMEM((px, ch, inner), F32),
            pltpu.VMEM((n_red * rows, 2 * cin), BF16),
            pltpu.VMEM((group * rows, 2 * cin), BF16),
            pltpu.VMEM((rows, 2 * cin), BF16),
            pltpu.VMEM((n_red * rows, 2 * cin), BF16),
            dma((16,)), dma((16,)), dma((4,)), dma((4,)), dma, dma, dma((8,)), dma((8,)),
            dma((px,)), dma((px,)), dma((2,)), dma((2,)),
            pltpu.SemaphoreType.REGULAR((max(1, max(n_gx, n_gy) - 2),)),
        ],
        compiler_params=pltpu.CompilerParams(
            collective_id=0, has_side_effects=True, vmem_limit_bytes=24 * 1024 * 1024),
    )(*[pltpu.with_memory_space_constraint(v, pltpu.HBM) for v in (activations, filters.reshape(3, 9 * ch, cin), conv_bias.reshape(1, ch), grad_output)])
    input_grads, filter_grads, bias_grads = pl.pallas_call(
        functools.partial(unpack, (ch, cin)),
        out_shape=(jax.ShapeDtypeStruct(activations.shape, BF16),
                   jax.ShapeDtypeStruct((3, 9 * ch, cin), F32),
                   jax.ShapeDtypeStruct((1, ch), F32)),
        in_specs=[vmem] * 2,
        out_specs=(hbm,) * 3,
        scratch_shapes=[pltpu.VMEM((3, 9 * ch, cin), F32), pltpu.VMEM((1, ch), F32), dma((3,))],
        compiler_params=pltpu.CompilerParams(vmem_limit_bytes=8 * 1024 * 1024),
    )(igrad, packed)
    return (input_grads, filter_grads.reshape(filters.shape), bias_grads.reshape(ch))


def solution(mesh):
    return jax.shard_map(
        per_device,
        mesh=mesh,
        in_specs=(
            P("af", "gx", "gy", None),
            P(None, None, None, "af", None),
            P("af"),
            P("af", "gx", "gy", None),
        ),
        out_specs=(P("af", "gx", "gy", None), P(None, None, None, "af", None), P("af")),
        check_vma=False,
    )
```

```python
import functools
import math

import jax
import jax.numpy as jnp
from jax import lax
from jax.experimental import pallas as pl
from jax.experimental.pallas import tpu as pltpu
from jax.sharding import PartitionSpec as P

MESH = pl.DeviceIdType.MESH
F32, BF16 = jnp.float32, jnp.bfloat16
SIDES = [(dx, dy) for dx in (-1, 0, 1) for dy in (-1, 0, 1) if (dx, dy) != (0, 0)]


def kernel(sizes, act_hbm, filt_hbm, bias_hbm, gout_hbm, igrad_ref, fgrad_ref,
           act_ref, filt_ref, bias_ref, gout_ref, filt_in, bias_in, gout_in, load_sem, acts, gate, gout, gate_k, w_fwd, w_flip, w_bwd, part, ig_out, ig_in, pack, pack_in, mine, total,
           a_send, a_recv, c_send, c_recv, g_send, g_recv, q_send, q_recv, r_send, r_recv, t_send, t_recv, near):
    n_gx, n_gy, px, py, nz, ch, rows, n_red, factor = sizes
    cin = 2 * ch
    inner = py * nz
    gx, gy, af = lax.axis_index("gx"), lax.axis_index("gy"), lax.axis_index("af")
    other = 1 - af
    group = n_gx * n_gy
    me = gx * n_gy + gy
    rounds = max(n_gx, n_gy) - 2
    core0, core1 = af == 0, af == 1

    loads = [pltpu.make_async_copy(src, dst, load_sem.at[at]) for at, (src, dst) in enumerate((
        (act_hbm, act_ref), (filt_hbm, filt_ref), (bias_hbm, bias_ref), (gout_hbm, gout_ref)))]
    for load in loads:
        load.start()

    def there(d):
        return (gx + d[0] >= 0) & (gx + d[0] < n_gx) & (gy + d[1] >= 0) & (gy + d[1] < n_gy)

    def back(d):
        return there((-d[0], -d[1]))

    barrier = pltpu.get_barrier_semaphore()
    around = sum(there(d).astype(jnp.int32) for d in SIDES)
    for d in SIDES:
        @pl.when(there(d))
        def _():
            pl.semaphore_signal(
                barrier, inc=1, device_id=(gx + d[0], gy + d[1], 1), device_id_type=MESH)

        @pl.when(there(d) & core1)
        def _():
            pl.semaphore_signal(
                barrier, inc=1, device_id=(gx + d[0], gy + d[1], 0), device_id_type=MESH)
    pl.semaphore_signal(barrier, inc=1, device_id=(gx, gy, other), device_id_type=MESH)

    def tell(at):
        for d in SIDES:
            @pl.when(there(d))
            def _():
                pl.semaphore_signal(
                    near.at[at], inc=1, device_id=(gx + d[0], gy + d[1], 1), device_id_type=MESH)

    def hear(at):
        pl.semaphore_wait(near.at[at], around)

    def spans(d):
        dx, dy = d
        sx = {1: (px, 1), -1: (1, 1), 0: (1, px)}[dx]
        tx = {1: (0, 1), -1: (px + 1, 1), 0: (1, px)}[dx]
        sy = {1: (py, 1), -1: (1, 1), 0: (1, py)}[dy]
        ty = {1: (0, 1), -1: (py + 1, 1), 0: (1, py)}[dy]
        lanes = lambda s: pl.ds(s[0] * nz, s[1] * nz)
        return (pl.ds(*sx), lanes(sy)), (pl.ds(*tx), lanes(ty))

    for d in SIDES:
        tx, tl = spans(d)[1]

        @pl.when(~back(d) & core0)
        def _():
            gate[tx, :, tl] = jnp.zeros((tx.size, cin, tl.size), BF16)

        @pl.when(~back(d) & core1)
        def _():
            acts[tx, :, :, tl] = jnp.zeros((tx.size, 2, ch, tl.size), BF16)

    loads[0].wait()
    for xo in range(px):
        acts[xo + 1, pl.ds(af, 1), :, nz:nz + inner] = (
            act_ref[:, xo].reshape(1, ch, inner))
    pl.semaphore_wait(barrier, around * (1 + af) + 1)

    def act_copy(s, half):
        d = SIDES[s]
        (sx, sl), (tx, tl) = spans(d)
        return pltpu.make_async_remote_copy(
            src_ref=acts.at[sx, half, :, sl], dst_ref=acts.at[tx, half, :, tl],
            send_sem=a_send.at[s], recv_sem=a_recv.at[2 * s + half],
            device_id=(gx + d[0], gy + d[1], 1), device_id_type=MESH)

    def gate_copy(s):
        d = SIDES[s]
        (sx, sl), (tx, tl) = spans(d)
        return pltpu.make_async_remote_copy(
            src_ref=gate.at[sx, :, sl], dst_ref=gate.at[tx, :, tl],
            send_sem=g_send.at[s], recv_sem=g_recv.at[s],
            device_id=(gx + d[0], gy + d[1], 0), device_id_type=MESH)

    def across(at, src, dst):
        return pltpu.make_async_remote_copy(
            src_ref=src, dst_ref=dst, send_sem=c_send.at[at], recv_sem=c_recv.at[at],
            device_id=(gx, gy, other), device_id_type=MESH)

    block = acts.at[pl.ds(1, px), 0, :, pl.ds(nz, inner)]
    act_over = across(0, block, block)
    filt_over = across(1, filt_ref, filt_in)
    bias_over = across(2, bias_ref, bias_in)
    gout_over = across(3, gout_ref, gout_in)
    block = gate.at[pl.ds(1, px), :, pl.ds(nz, inner)]
    gate_over = across(4, block, block)

    def ig_over(xo):
        return pltpu.make_async_remote_copy(
            src_ref=ig_out.at[:, xo], dst_ref=ig_in.at[:, xo],
            send_sem=q_send.at[xo], recv_sem=q_recv.at[xo],
            device_id=(gx, gy, other), device_id_type=MESH)

    order = sorted(range(8), key=lambda s: (SIDES[s][0] == 0) * 2 + (SIDES[s][1] == 0))
    for s in order:
        @pl.when(there(SIDES[s]))
        def _():
            act_copy(s, af).start()

    @pl.when(core0)
    def _():
        act_over.start()

    if rounds > 0:
        @pl.when(core1)
        def _():
            tell(0)

    for load in loads[1:]:
        load.wait()
    filt_over.start()

    lane = lax.broadcasted_iota(jnp.int32, (1, nz), 1)

    def from_below(v):
        return jnp.where(lane == 0, 0.0, pltpu.roll(v, 1, 1))

    def from_above(v):
        return jnp.where(lane == nz - 1, 0.0, pltpu.roll(v, nz - 1, 1))

    step = 2 if py % 2 == 0 else 1
    head = ch
    main, fold = 3 * ch, 3 * ch // 2
    wide = lax.broadcasted_iota(jnp.int32, (1, 2 * cin), 1)

    def two_parts(v):
        high = v.astype(BF16).astype(F32)
        return jnp.where(wide < cin, high, v - high)

    def settle(ref, count, sem):
        block = ref.at[pl.ds(0, count * rows)]
        return pltpu.make_async_copy(block, block, sem)

    low = (n_gx - 1) // 2 * n_gy
    high = low + n_gy if n_gx > 1 else low
    pairs = n_gy // 2
    homes = [(low, high)[b % 2] + b // 2 % pairs * 2 for b in range(n_red)]
    turns = [b // 2 // pairs for b in range(n_red)]
    n_turns = turns[-1] + 1

    def scatter(first, count):
        for b in range(first, first + count):
            for h in range(2):
                chip = homes[b] + h
                block = pack.at[pl.ds((h * n_red + b) * rows, rows)]
                slot = pack_in.at[turns[b], pl.ds(pl.multiple_of(me * rows, 16), rows)]
                came = r_recv.at[turns[b]]

                @pl.when(me == chip)
                def _():
                    pltpu.make_async_copy(block, slot, came).start()

                @pl.when(me != chip)
                def _():
                    pltpu.make_async_remote_copy(
                        src_ref=block, dst_ref=slot, send_sem=r_send, recv_sem=came,
                        device_id=(chip // n_gy, chip % n_gy, 1), device_id_type=MESH).start()

    half = lax.rem(me, 2)
    at_block, has = [], []
    for turn in range(n_turns):
        at, found = jnp.int32(0), jnp.int32(0)
        for b in range(n_red):
            if turns[b] == turn:
                hit = (me - half == homes[b]).astype(jnp.int32)
                at, found = at + b * hit, found + hit
        at_block.append(pl.multiple_of(at * rows, 16))
        has.append(core1 & (found > 0))

    def share(turn, peer):
        own = (half == 1) & (peer == me)
        place = total.at[pl.ds(at_block[turn], rows)]

        @pl.when(own)
        def _():
            pltpu.make_async_copy(mine.at[turn], place, t_recv).start()

        @pl.when(~own)
        def _():
            pltpu.make_async_remote_copy(
                src_ref=mine.at[turn], dst_ref=place, send_sem=t_send.at[turn], recv_sem=t_recv,
                device_id=(peer // n_gy, peer % n_gy, half), device_id_type=MESH).start()

    @pl.when(core1)
    def _():
        for i in range(3):
            for j in range(3):
                w_fwd[j, 3 * ch:6 * ch, i * cin:(i + 1) * cin] = filt_ref[i, j * 3 * ch:(j + 1) * 3 * ch, :]
        for xo in range(px):
            gout[xo, ch:2 * ch] = gout_ref[:, xo].reshape(ch, inner)
        filt_over.wait_recv()
        for i in range(3):
            for j in range(3):
                w_fwd[j, 0:3 * ch, i * cin:(i + 1) * cin] = filt_in[i, j * 3 * ch:(j + 1) * 3 * ch, :]
        bias_over.wait_recv()
        gout_over.wait_recv()
        for xo in range(px):
            gout[xo, 0:ch] = gout_in[:, xo].reshape(ch, inner)
        eye = (lax.broadcasted_iota(jnp.int32, (ch, ch), 0)
               == lax.broadcasted_iota(jnp.int32, (ch, ch), 1))
        bias = [jnp.sum(jnp.where(eye, ref[...], 0.0), axis=1, keepdims=True) for ref in (bias_in, bias_ref)]
        for at in range(1, rounds):
            hear(at - 1)
            tell(at)

        act_over.wait_recv()
        for s in reversed(order):
            @pl.when(back(SIDES[s]))
            def _():
                for h in range(2):
                    act_copy(s, h).wait_recv()

        sums = [jnp.zeros((ch, nz), F32)] * 2
        for xo in range(px):
            for y0 in range(0, py, step):
                acc = None
                for j in range(3):
                    window = acts[xo:xo + 3, :, :, (y0 + j) * nz:(y0 + j + step) * nz]
                    term = jnp.dot(w_fwd[j], window.reshape(3 * cin, step * nz),
                                   preferred_element_type=F32)
                    acc = term if acc is None else acc + term
                for h in range(2):
                    for u in range(step):
                        cut = acc[3 * h * ch:3 * (h + 1) * ch, u * nz:(u + 1) * nz]
                        pre = (cut[ch:2 * ch] + from_below(cut[:ch]) + from_above(cut[2 * ch:])) + bias[h]
                        lanes = slice((y0 + u) * nz, (y0 + u + 1) * nz)
                        squash = 1.0 / (1.0 + jnp.exp(-pre))
                        g = gout[xo, h * ch:(h + 1) * ch, lanes].astype(F32) * squash * (1.0 + pre * (1.0 - squash))
                        rounded = g.astype(BF16)
                        g = rounded.astype(F32)
                        sums[h] = sums[h] + g
                        gate[xo + 1, h * ch:(h + 1) * ch, (y0 + u + 1) * nz:(y0 + u + 2) * nz] = rounded
                        at = 3 * h * ch
                        gate_k[xo, at:at + ch, lanes] = from_above(g).astype(BF16)
                        gate_k[xo, at + ch:at + 2 * ch, lanes] = rounded
                        gate_k[xo, at + 2 * ch:at + 3 * ch, lanes] = from_below(g).astype(BF16)

        used = head + 3 * (main + fold)
        for h in range(2):
            first = h * n_red * rows
            whole = jnp.sum(sums[h], axis=1, keepdims=True) * factor + jnp.zeros((ch, 2 * cin), F32)
            pack[first:first + head, :] = two_parts(whole).astype(BF16)
            if n_red * rows > used:
                pack[first + used:first + n_red * rows, :] = jnp.zeros((n_red * rows - used, 2 * cin), BF16)

        ready = 0
        for j in range(3):
            both = None
            for xo in range(px):
                window = acts[xo:xo + 3, :, :, j * nz:j * nz + inner].reshape(3 * cin, inner)
                term = lax.dot_general(gate_k[xo], window, (((1,), (1,)), ((), ())),
                                       preferred_element_type=F32)
                both = term if both is None else both + term
            both = (both * factor).astype(BF16)
            for h in range(2):
                acc = both[3 * h * ch:3 * (h + 1) * ch]
                base = h * n_red * rows + head + j * (main + fold)
                pack[base:base + main, :] = acc[:, :2 * cin]
                pack[base + main:base + main + fold, 0:cin] = acc[:fold, 2 * cin:]
                pack[base + main:base + main + fold, cin:2 * cin] = acc[fold:, 2 * cin:]
            if j == 0 and rounds > 0:
                hear(rounds - 1)
            done = n_red if j == 2 else (head + (j + 1) * (main + fold)) // rows
            if done > ready:
                scatter(ready, done - ready)
            ready = done

        gate_over.start()
        for s in order:
            @pl.when(there(SIDES[s]))
            def _():
                gate_copy(s).start()

    @pl.when(core0)
    def _():
        bias_over.start()
        gout_over.start()
        filt_over.wait_recv()
        for i in range(3):
            for j in range(3):
                for k in range(3):
                    at = (3 * j + k) * ch
                    to = (2 - i) * cin
                    w_flip[j, to:to + ch, k * cin:(k + 1) * cin] = filt_ref[i, at:at + ch, :]
                    w_flip[j, to + ch:to + cin, k * cin:(k + 1) * cin] = filt_in[i, at:at + ch, :]
        for j in range(3):
            w_bwd[j] = w_flip[j].astype(F32).T.astype(BF16)

        gate_over.wait_recv()
        for s in order:
            @pl.when(back(SIDES[s]))
            def _():
                gate_copy(s).wait_recv()
        for xo in range(px):
            for y0 in range(0, py, step):
                acc = None
                for j in range(3):
                    at = y0 + 2 - j
                    window = gate[xo:xo + 3, :, at * nz:(at + step) * nz].reshape(3 * cin, step * nz)
                    term = jnp.dot(w_bwd[j], window, preferred_element_type=F32)
                    acc = term if acc is None else acc + term
                for u in range(step):
                    cut = acc[:, u * nz:(u + 1) * nz]
                    full = (cut[cin:2 * cin] + from_above(cut[:cin]) + from_below(cut[2 * cin:]))
                    part[xo, :, :, (y0 + u) * nz:(y0 + u + 1) * nz] = full.reshape(2, ch, nz)
            ig_out[:, xo] = part[xo, 1].reshape(ch, py, nz).astype(BF16)
            ig_over(xo).start()
            igrad_ref[:, xo] = part[xo, 0].reshape(ch, py, nz).astype(BF16)

    for turn in range(n_turns):
        @pl.when(has[turn])
        def _():
            settle(pack_in.at[turn], group, r_recv.at[turn]).wait()

            def add(t, v):
                return v + pack_in[turn, pl.ds(pl.multiple_of(t * rows, 16), rows), :].astype(F32)

            summed = pack_in[turn, 0:rows, :].astype(F32)
            if group <= 32:
                for t in range(1, group):
                    summed = add(t, summed)
            else:
                summed = lax.fori_loop(1, group, add, summed)
            both = two_parts(summed + pltpu.roll(summed, cin, 1))
            at = at_block[turn] + lax.broadcasted_iota(jnp.int32, (rows, 1), 0)
            mine[turn] = jnp.where(at < head, both, summed).astype(BF16)
            if group <= 32:
                for peer in range(group):
                    share(turn, peer)
            else:
                lax.fori_loop(0, group, lambda peer, _: share(turn, peer) or 0, 0)

    for s in order:
        @pl.when(there(SIDES[s]))
        def _():
            act_copy(s, af).wait_send()

        @pl.when(there(SIDES[s]) & core1)
        def _():
            gate_copy(s).wait_send()
    filt_over.wait_send()

    @pl.when(core0)
    def _():
        act_over.wait_send()
        bias_over.wait_send()
        gout_over.wait_send()
        for xo in range(px):
            ig_over(xo).wait_send()

    @pl.when(core1)
    def _():
        gate_over.wait_send()
        for xo in range(px):
            ig_over(xo).wait_recv()
        igrad_ref[...] = ig_in[...]

    kept = sum(v.astype(jnp.int32) for v in has)
    for count in range(n_turns + 1):
        @pl.when(core1 & (kept == count))
        def _():
            settle(pack, 2 * n_red - count, r_send).wait()

    for turn in range(n_turns):
        @pl.when(has[turn] & (half == 1))
        def _():
            settle(pack_in.at[turn], group - 1, t_send.at[turn]).wait()

        @pl.when(has[turn] & (half == 0))
        def _():
            settle(pack_in.at[turn], group, t_send.at[turn]).wait()

    settle(total, n_red, t_recv).wait()
    fgrad_ref[...] = total[...]


def unpack(sizes, igrad_ref, packed, igrad_out, fgrad_out, bias_out, taps, bias, sems):
    ch, cin = sizes
    early = pltpu.make_async_copy(igrad_ref, igrad_out, sems.at[0])
    early.start()
    head, main, fold = ch, 3 * ch, 3 * ch // 2
    column = (packed[0:head, :].astype(F32) + pltpu.roll(packed[0:head, :].astype(F32), cin, 1))[:, :1]
    eye = (lax.broadcasted_iota(jnp.int32, (ch, ch), 0)
           == lax.broadcasted_iota(jnp.int32, (ch, ch), 1))
    bias[...] = jnp.sum(jnp.where(eye, column, 0.0), axis=0, keepdims=True)
    small = pltpu.make_async_copy(bias, bias_out, sems.at[1])
    small.start()
    for j in range(3):
        base = head + j * (main + fold)
        block = packed[base:base + main + fold, :].astype(F32)
        at = j * main
        taps[0, at:at + main, :] = block[:main, :cin]
        taps[1, at:at + main, :] = block[:main, cin:]
        taps[2, at:at + fold, :] = block[main:, :cin]
        taps[2, at + fold:at + main, :] = block[main:, cin:]
    large = pltpu.make_async_copy(taps, fgrad_out, sems.at[2])
    large.start()
    early.wait()
    small.wait()
    large.wait()


def per_device(activations, filters, conv_bias, grad_output):
    ch, px, py, nz = activations.shape
    n_gx, n_gy = lax.axis_size("gx"), lax.axis_size("gy")
    group = n_gx * n_gy
    cin = 2 * ch
    inner = py * nz
    factor = 1.0 / math.sqrt(px * n_gx * py * n_gy * nz)
    used = ch + 3 * (3 * ch + 3 * ch // 2)
    rows = 16 * (-(-(used // 16) // 6))
    n_red = -(-used // rows)
    n_turns = (n_red - 1) // 2 // (n_gy // 2) + 1

    vmem = pl.BlockSpec(memory_space=pltpu.VMEM)
    hbm = pl.BlockSpec(memory_space=pltpu.HBM)
    dma = pltpu.SemaphoreType.DMA
    igrad, packed = pl.pallas_call(
        functools.partial(kernel, (n_gx, n_gy, px, py, nz, ch, rows, n_red, factor)),
        out_shape=(jax.ShapeDtypeStruct((ch, px, py, nz), BF16),
                   jax.ShapeDtypeStruct((n_red * rows, 2 * cin), BF16)),
        in_specs=[hbm] * 4,
        out_specs=(vmem, vmem),
        scratch_shapes=[
            pltpu.VMEM((ch, px, py, nz), BF16),
            pltpu.VMEM((3, 9 * ch, cin), BF16),
            pltpu.VMEM((1, ch), F32),
            pltpu.VMEM((ch, px, py, nz), BF16),
            pltpu.VMEM((3, 9 * ch, cin), BF16),
            pltpu.VMEM((1, ch), F32),
            pltpu.VMEM((ch, px, py, nz), BF16),
            dma((4,)),
            pltpu.VMEM((px + 2, 2, ch, (py + 2) * nz), BF16),
            pltpu.VMEM((px + 2, cin, (py + 2) * nz), BF16),
            pltpu.VMEM((px, cin, inner), BF16),
            pltpu.VMEM((px, 3 * cin, inner), BF16),
            pltpu.VMEM((3, 3 * cin, 3 * cin), BF16),
            pltpu.VMEM((3, 3 * cin, 3 * cin), BF16),
            pltpu.VMEM((3, 3 * cin, 3 * cin), BF16),
            pltpu.VMEM((px, 2, ch, inner), F32),
            pltpu.VMEM((ch, px, py, nz), BF16),
            pltpu.VMEM((ch, px, py, nz), BF16),
            pltpu.VMEM((2 * n_red * rows, 2 * cin), BF16),
            pltpu.VMEM((n_turns, group * rows, 2 * cin), BF16),
            pltpu.VMEM((n_turns, rows, 2 * cin), BF16),
            pltpu.VMEM((n_red * rows, 2 * cin), BF16),
            dma((8,)), dma((16,)), dma((5,)), dma((5,)), dma((8,)), dma((8,)),
            dma((px,)), dma((px,)), dma, dma((n_turns,)), dma((n_turns,)), dma,
            pltpu.SemaphoreType.REGULAR((max(1, max(n_gx, n_gy) - 2),)),
        ],
        compiler_params=pltpu.CompilerParams(
            collective_id=0, has_side_effects=True, vmem_limit_bytes=24 * 1024 * 1024),
    )(*[pltpu.with_memory_space_constraint(v, pltpu.HBM) for v in (activations, filters.reshape(3, 9 * ch, cin), conv_bias.reshape(1, ch), grad_output)])
    input_grads, filter_grads, bias_grads = pl.pallas_call(
        functools.partial(unpack, (ch, cin)),
        out_shape=(jax.ShapeDtypeStruct(activations.shape, BF16),
                   jax.ShapeDtypeStruct((3, 9 * ch, cin), F32),
                   jax.ShapeDtypeStruct((1, ch), F32)),
        in_specs=[vmem] * 2,
        out_specs=(hbm,) * 3,
        scratch_shapes=[pltpu.VMEM((3, 9 * ch, cin), F32), pltpu.VMEM((1, ch), F32), dma((3,))],
        compiler_params=pltpu.CompilerParams(vmem_limit_bytes=8 * 1024 * 1024),
    )(igrad, packed)
    return (input_grads, filter_grads.reshape(filters.shape), bias_grads.reshape(ch))


def solution(mesh):
    return jax.shard_map(
        per_device,
        mesh=mesh,
        in_specs=(
            P("af", "gx", "gy", None),
            P(None, None, None, "af", None),
            P("af"),
            P("af", "gx", "gy", None),
        ),
        out_specs=(P("af", "gx", "gy", None), P(None, None, None, "af", None), P("af")),
        check_vma=False,
    )
```

```python
import functools
import math

import jax
import jax.numpy as jnp
from jax import lax
from jax.experimental import pallas as pl
from jax.experimental.pallas import tpu as pltpu
from jax.sharding import PartitionSpec as P

MESH = pl.DeviceIdType.MESH
F32, BF16 = jnp.float32, jnp.bfloat16
SIDES = [(dx, dy) for dx in (-1, 0, 1) for dy in (-1, 0, 1) if (dx, dy) != (0, 0)]
EARLY = [s for s, (dx, dy) in enumerate(SIDES) if dx <= 0]


def kernel(sizes, act_hbm, filt_hbm, bias_hbm, gout_hbm, igrad_ref, fgrad_ref,
           act_ref, filt_ref, bias_ref, gout_ref, filt_in, bias_in, gout_in, load_sem, acts, gate, gout, gate_k, w_fwd, w_flip, w_bwd, part, ig_out, ig_in, pack, pack_in, mine, total,
           a_send, a_recv, c_send, c_recv, g_send, g_recv, q_send, q_recv, r_send, r_recv, t_send, t_recv, near):
    n_gx, n_gy, px, py, nz, ch, rows, n_red, factor = sizes
    cin = 2 * ch
    inner = py * nz
    gx, gy, af = lax.axis_index("gx"), lax.axis_index("gy"), lax.axis_index("af")
    other = 1 - af
    group = n_gx * n_gy
    me = gx * n_gy + gy
    rounds = max(1, max(n_gx, n_gy) - 2)
    core0, core1 = af == 0, af == 1

    loads = [pltpu.make_async_copy(src, dst, load_sem.at[at]) for at, (src, dst) in enumerate((
        (act_hbm, act_ref), (filt_hbm, filt_ref), (bias_hbm, bias_ref), (gout_hbm, gout_ref)))]
    for load in loads:
        load.start()

    def there(d):
        return (gx + d[0] >= 0) & (gx + d[0] < n_gx) & (gy + d[1] >= 0) & (gy + d[1] < n_gy)

    def back(d):
        return there((-d[0], -d[1]))

    barrier = pltpu.get_barrier_semaphore()
    around = sum(there(d).astype(jnp.int32) for d in SIDES)
    before = sum(there(SIDES[s]).astype(jnp.int32) for s in EARLY)

    def greet(d, core):
        pl.semaphore_signal(
            barrier, inc=1, device_id=(gx + d[0], gy + d[1], core), device_id_type=MESH)

    @pl.when(core1)
    def _():
        for d in SIDES:
            @pl.when(there(d))
            def _():
                greet(d, 1)
        for s in EARLY:
            @pl.when(back(SIDES[s]))
            def _():
                greet((-SIDES[s][0], -SIDES[s][1]), 0)

    pl.semaphore_signal(barrier, inc=1, device_id=(gx, gy, other), device_id_type=MESH)

    def tell(at):
        for d in SIDES:
            @pl.when(there(d))
            def _():
                pl.semaphore_signal(
                    near.at[at], inc=1, device_id=(gx + d[0], gy + d[1], 1), device_id_type=MESH)

    def hear(at):
        pl.semaphore_wait(near.at[at], around)

    def spans(d):
        dx, dy = d
        sx = {1: (px, 1), -1: (1, 1), 0: (1, px)}[dx]
        tx = {1: (0, 1), -1: (px + 1, 1), 0: (1, px)}[dx]
        sy = {1: (py, 1), -1: (1, 1), 0: (1, py)}[dy]
        ty = {1: (0, 1), -1: (py + 1, 1), 0: (1, py)}[dy]
        lanes = lambda s: pl.ds(s[0] * nz, s[1] * nz)
        return (pl.ds(*sx), lanes(sy)), (pl.ds(*tx), lanes(ty))

    for d in SIDES:
        tx, tl = spans(d)[1]

        @pl.when(~back(d) & core0)
        def _():
            gate[tx, :, tl] = jnp.zeros((tx.size, cin, tl.size), BF16)

        @pl.when(~back(d) & core1)
        def _():
            acts[tx, :, :, tl] = jnp.zeros((tx.size, 2, ch, tl.size), BF16)

    loads[0].wait()
    for xo in range(px):
        acts[xo + 1, pl.ds(af, 1), :, nz:nz + inner] = (
            act_ref[:, xo].reshape(1, ch, inner))
    pl.semaphore_wait(barrier, around * af + before * other + 1)

    def act_copy(s, half):
        d = SIDES[s]
        (sx, sl), (tx, tl) = spans(d)
        return pltpu.make_async_remote_copy(
            src_ref=acts.at[sx, half, :, sl], dst_ref=acts.at[tx, half, :, tl],
            send_sem=a_send.at[2 * s + half], recv_sem=a_recv.at[2 * s + half],
            device_id=(gx + d[0], gy + d[1], 1), device_id_type=MESH)

    def gate_copy(s):
        d = SIDES[s]
        (sx, sl), (tx, tl) = spans(d)
        return pltpu.make_async_remote_copy(
            src_ref=gate.at[sx, :, sl], dst_ref=gate.at[tx, :, tl],
            send_sem=g_send.at[s], recv_sem=g_recv.at[s],
            device_id=(gx + d[0], gy + d[1], 0), device_id_type=MESH)

    def across(at, src, dst):
        return pltpu.make_async_remote_copy(
            src_ref=src, dst_ref=dst, send_sem=c_send.at[at], recv_sem=c_recv.at[at],
            device_id=(gx, gy, other), device_id_type=MESH)

    block = acts.at[pl.ds(1, px), 0, :, pl.ds(nz, inner)]
    act_over = across(0, block, block)
    filt_over = across(1, filt_ref, filt_in)
    bias_over = across(2, bias_ref, bias_in)
    gout_over = across(3, gout_ref, gout_in)
    block = gate.at[pl.ds(1, px), :, pl.ds(nz, inner)]
    gate_over = across(4, block, block)

    def ig_over(xo):
        return pltpu.make_async_remote_copy(
            src_ref=ig_out.at[:, xo], dst_ref=ig_in.at[:, xo],
            send_sem=q_send.at[xo], recv_sem=q_recv.at[xo],
            device_id=(gx, gy, other), device_id_type=MESH)

    order = sorted(range(8), key=lambda s: (SIDES[s][0] == 0) * 2 + (SIDES[s][1] == 0))
    @pl.when(core0)
    def _():
        for s in order:
            if s in EARLY:
                @pl.when(there(SIDES[s]))
                def _():
                    act_copy(s, 0).start()
        act_over.start()

    @pl.when(core1)
    def _():
        for s in order:
            @pl.when(there(SIDES[s]))
            def _():
                act_copy(s, 1).start()
        act_over.wait_recv()
        for s in order:
            if s not in EARLY:
                @pl.when(there(SIDES[s]))
                def _():
                    act_copy(s, 0).start()
        tell(0)

    for load in loads[1:]:
        load.wait()
    filt_over.start()

    lane = lax.broadcasted_iota(jnp.int32, (1, nz), 1)

    def from_below(v):
        return jnp.where(lane == 0, 0.0, pltpu.roll(v, 1, 1))

    def from_above(v):
        return jnp.where(lane == nz - 1, 0.0, pltpu.roll(v, nz - 1, 1))

    step = 2 if py % 2 == 0 else 1
    head = ch
    main, fold = 3 * ch, 3 * ch // 2
    wide = lax.broadcasted_iota(jnp.int32, (1, 2 * cin), 1)

    def two_parts(v):
        high = v.astype(BF16).astype(F32)
        return jnp.where(wide < cin, high, v - high)

    def settle(ref, count, sem):
        block = ref.at[pl.ds(0, count * rows)]
        return pltpu.make_async_copy(block, block, sem)

    low = (n_gx - 1) // 2 * n_gy
    high = low + n_gy if n_gx > 1 else low
    pairs = n_gy // 2
    homes = [(low, high)[b % 2] + b // 2 % pairs * 2 for b in range(n_red)]
    turns = [b // 2 // pairs for b in range(n_red)]
    n_turns = turns[-1] + 1

    def scatter(first, count):
        for b in range(first, first + count):
            for h in range(2):
                chip = homes[b] + h
                block = pack.at[pl.ds((h * n_red + b) * rows, rows)]
                slot = pack_in.at[turns[b], pl.ds(pl.multiple_of(me * rows, 16), rows)]
                came = r_recv.at[turns[b]]

                @pl.when(me == chip)
                def _():
                    pltpu.make_async_copy(block, slot, came).start()

                @pl.when(me != chip)
                def _():
                    pltpu.make_async_remote_copy(
                        src_ref=block, dst_ref=slot, send_sem=r_send, recv_sem=came,
                        device_id=(chip // n_gy, chip % n_gy, 1), device_id_type=MESH).start()

    half = lax.rem(me, 2)
    at_block, has = [], []
    for turn in range(n_turns):
        at, found = jnp.int32(0), jnp.int32(0)
        for b in range(n_red):
            if turns[b] == turn:
                hit = (me - half == homes[b]).astype(jnp.int32)
                at, found = at + b * hit, found + hit
        at_block.append(pl.multiple_of(at * rows, 16))
        has.append(core1 & (found > 0))

    def share(turn, peer):
        own = (half == 1) & (peer == me)
        place = total.at[pl.ds(at_block[turn], rows)]

        @pl.when(own)
        def _():
            pltpu.make_async_copy(mine.at[turn], place, t_recv).start()

        @pl.when(~own)
        def _():
            pltpu.make_async_remote_copy(
                src_ref=mine.at[turn], dst_ref=place, send_sem=t_send.at[turn], recv_sem=t_recv,
                device_id=(peer // n_gy, peer % n_gy, half), device_id_type=MESH).start()

    @pl.when(core1)
    def _():
        for i in range(3):
            for j in range(3):
                w_fwd[j, 3 * ch:6 * ch, i * cin:(i + 1) * cin] = filt_ref[i, j * 3 * ch:(j + 1) * 3 * ch, :]
        for xo in range(px):
            gout[xo, ch:2 * ch] = gout_ref[:, xo].reshape(ch, inner)
        filt_over.wait_recv()
        for i in range(3):
            for j in range(3):
                w_fwd[j, 0:3 * ch, i * cin:(i + 1) * cin] = filt_in[i, j * 3 * ch:(j + 1) * 3 * ch, :]
        bias_over.wait_recv()
        gout_over.wait_recv()
        for xo in range(px):
            gout[xo, 0:ch] = gout_in[:, xo].reshape(ch, inner)
        eye = (lax.broadcasted_iota(jnp.int32, (ch, ch), 0)
               == lax.broadcasted_iota(jnp.int32, (ch, ch), 1))
        bias = [jnp.sum(jnp.where(eye, ref[...], 0.0), axis=1, keepdims=True) for ref in (bias_in, bias_ref)]
        for at in range(1, rounds):
            hear(at - 1)
            tell(at)

        for s in reversed(order):
            @pl.when(back(SIDES[s]))
            def _():
                for h in range(2):
                    act_copy(s, h).wait_recv()

        sums = [jnp.zeros((ch, nz), F32)] * 2
        for xo in range(px):
            for y0 in range(0, py, step):
                acc = None
                for j in range(3):
                    window = acts[xo:xo + 3, :, :, (y0 + j) * nz:(y0 + j + step) * nz]
                    term = jnp.dot(w_fwd[j], window.reshape(3 * cin, step * nz),
                                   preferred_element_type=F32)
                    acc = term if acc is None else acc + term
                for h in range(2):
                    for u in range(step):
                        cut = acc[3 * h * ch:3 * (h + 1) * ch, u * nz:(u + 1) * nz]
                        pre = (cut[ch:2 * ch] + from_below(cut[:ch]) + from_above(cut[2 * ch:])) + bias[h]
                        lanes = slice((y0 + u) * nz, (y0 + u + 1) * nz)
                        squash = 1.0 / (1.0 + jnp.exp(-pre))
                        g = gout[xo, h * ch:(h + 1) * ch, lanes].astype(F32) * squash * (1.0 + pre * (1.0 - squash))
                        rounded = g.astype(BF16)
                        g = rounded.astype(F32)
                        sums[h] = sums[h] + g
                        gate[xo + 1, h * ch:(h + 1) * ch, (y0 + u + 1) * nz:(y0 + u + 2) * nz] = rounded
                        at = 3 * h * ch
                        gate_k[xo, at:at + ch, lanes] = from_above(g).astype(BF16)
                        gate_k[xo, at + ch:at + 2 * ch, lanes] = rounded
                        gate_k[xo, at + 2 * ch:at + 3 * ch, lanes] = from_below(g).astype(BF16)

        used = head + 3 * (main + fold)
        for h in range(2):
            first = h * n_red * rows
            whole = jnp.sum(sums[h], axis=1, keepdims=True) * factor + jnp.zeros((ch, 2 * cin), F32)
            pack[first:first + head, :] = two_parts(whole).astype(BF16)
            if n_red * rows > used:
                pack[first + used:first + n_red * rows, :] = jnp.zeros((n_red * rows - used, 2 * cin), BF16)

        ready = 0
        for j in range(3):
            both = None
            for xo in range(px):
                window = acts[xo:xo + 3, :, :, j * nz:j * nz + inner].reshape(3 * cin, inner)
                term = lax.dot_general(gate_k[xo], window, (((1,), (1,)), ((), ())),
                                       preferred_element_type=F32)
                both = term if both is None else both + term
            both = (both * factor).astype(BF16)
            for h in range(2):
                acc = both[3 * h * ch:3 * (h + 1) * ch]
                base = h * n_red * rows + head + j * (main + fold)
                pack[base:base + main, :] = acc[:, :2 * cin]
                pack[base + main:base + main + fold, 0:cin] = acc[:fold, 2 * cin:]
                pack[base + main:base + main + fold, cin:2 * cin] = acc[fold:, 2 * cin:]
            if j == 0:
                hear(rounds - 1)
            done = n_red if j == 2 else (head + (j + 1) * (main + fold)) // rows
            if done > ready:
                scatter(ready, done - ready)
            ready = done

        gate_over.start()
        for s in order:
            @pl.when(there(SIDES[s]))
            def _():
                gate_copy(s).start()

    @pl.when(core0)
    def _():
        bias_over.start()
        gout_over.start()
        filt_over.wait_recv()
        for i in range(3):
            for j in range(3):
                for k in range(3):
                    at = (3 * j + k) * ch
                    to = (2 - i) * cin
                    w_flip[j, to:to + ch, k * cin:(k + 1) * cin] = filt_ref[i, at:at + ch, :]
                    w_flip[j, to + ch:to + cin, k * cin:(k + 1) * cin] = filt_in[i, at:at + ch, :]
        for j in range(3):
            w_bwd[j] = w_flip[j].astype(F32).T.astype(BF16)

        gate_over.wait_recv()
        for s in order:
            @pl.when(back(SIDES[s]))
            def _():
                gate_copy(s).wait_recv()
        for xo in range(px):
            for y0 in range(0, py, step):
                acc = None
                for j in range(3):
                    at = y0 + 2 - j
                    window = gate[xo:xo + 3, :, at * nz:(at + step) * nz].reshape(3 * cin, step * nz)
                    term = jnp.dot(w_bwd[j], window, preferred_element_type=F32)
                    acc = term if acc is None else acc + term
                for u in range(step):
                    cut = acc[:, u * nz:(u + 1) * nz]
                    full = (cut[cin:2 * cin] + from_above(cut[:cin]) + from_below(cut[2 * cin:]))
                    part[xo, :, :, (y0 + u) * nz:(y0 + u + 1) * nz] = full.reshape(2, ch, nz)
            ig_out[:, xo] = part[xo, 1].reshape(ch, py, nz).astype(BF16)
            ig_over(xo).start()
            igrad_ref[:, xo] = part[xo, 0].reshape(ch, py, nz).astype(BF16)

    for turn in range(n_turns):
        @pl.when(has[turn])
        def _():
            settle(pack_in.at[turn], group, r_recv.at[turn]).wait()

            def add(t, v):
                return v + pack_in[turn, pl.ds(pl.multiple_of(t * rows, 16), rows), :].astype(F32)

            summed = pack_in[turn, 0:rows, :].astype(F32)
            if group <= 32:
                for t in range(1, group):
                    summed = add(t, summed)
            else:
                summed = lax.fori_loop(1, group, add, summed)
            both = two_parts(summed + pltpu.roll(summed, cin, 1))
            at = at_block[turn] + lax.broadcasted_iota(jnp.int32, (rows, 1), 0)
            mine[turn] = jnp.where(at < head, both, summed).astype(BF16)
            if group <= 32:
                for peer in range(group):
                    share(turn, peer)
            else:
                lax.fori_loop(0, group, lambda peer, _: share(turn, peer) or 0, 0)

    for s in order:
        @pl.when(there(SIDES[s]) & (core1 | (s in EARLY)))
        def _():
            act_copy(s, af).wait_send()

        @pl.when(there(SIDES[s]) & core1)
        def _():
            gate_copy(s).wait_send()
            if s not in EARLY:
                act_copy(s, 0).wait_send()
    filt_over.wait_send()

    @pl.when(core0)
    def _():
        act_over.wait_send()
        bias_over.wait_send()
        gout_over.wait_send()
        for xo in range(px):
            ig_over(xo).wait_send()

    @pl.when(core1)
    def _():
        gate_over.wait_send()
        for xo in range(px):
            ig_over(xo).wait_recv()
        igrad_ref[...] = ig_in[...]

    kept = sum(v.astype(jnp.int32) for v in has)
    for count in range(n_turns + 1):
        @pl.when(core1 & (kept == count))
        def _():
            settle(pack, 2 * n_red - count, r_send).wait()

    for turn in range(n_turns):
        @pl.when(has[turn] & (half == 1))
        def _():
            settle(pack_in.at[turn], group - 1, t_send.at[turn]).wait()

        @pl.when(has[turn] & (half == 0))
        def _():
            settle(pack_in.at[turn], group, t_send.at[turn]).wait()

    settle(total, n_red, t_recv).wait()
    fgrad_ref[...] = total[...]


def unpack(sizes, igrad_ref, packed, igrad_out, fgrad_out, bias_out, taps, bias, sems):
    ch, cin = sizes
    early = pltpu.make_async_copy(igrad_ref, igrad_out, sems.at[0])
    early.start()
    head, main, fold = ch, 3 * ch, 3 * ch // 2
    column = (packed[0:head, :].astype(F32) + pltpu.roll(packed[0:head, :].astype(F32), cin, 1))[:, :1]
    eye = (lax.broadcasted_iota(jnp.int32, (ch, ch), 0)
           == lax.broadcasted_iota(jnp.int32, (ch, ch), 1))
    bias[...] = jnp.sum(jnp.where(eye, column, 0.0), axis=0, keepdims=True)
    small = pltpu.make_async_copy(bias, bias_out, sems.at[1])
    small.start()
    for j in range(3):
        base = head + j * (main + fold)
        block = packed[base:base + main + fold, :].astype(F32)
        at = j * main
        taps[0, at:at + main, :] = block[:main, :cin]
        taps[1, at:at + main, :] = block[:main, cin:]
        taps[2, at:at + fold, :] = block[main:, :cin]
        taps[2, at + fold:at + main, :] = block[main:, cin:]
    large = pltpu.make_async_copy(taps, fgrad_out, sems.at[2])
    large.start()
    early.wait()
    small.wait()
    large.wait()


def per_device(activations, filters, conv_bias, grad_output):
    ch, px, py, nz = activations.shape
    n_gx, n_gy = lax.axis_size("gx"), lax.axis_size("gy")
    group = n_gx * n_gy
    cin = 2 * ch
    inner = py * nz
    factor = 1.0 / math.sqrt(px * n_gx * py * n_gy * nz)
    used = ch + 3 * (3 * ch + 3 * ch // 2)
    rows = 16 * (-(-(used // 16) // 6))
    n_red = -(-used // rows)
    n_turns = (n_red - 1) // 2 // (n_gy // 2) + 1

    vmem = pl.BlockSpec(memory_space=pltpu.VMEM)
    hbm = pl.BlockSpec(memory_space=pltpu.HBM)
    dma = pltpu.SemaphoreType.DMA
    igrad, packed = pl.pallas_call(
        functools.partial(kernel, (n_gx, n_gy, px, py, nz, ch, rows, n_red, factor)),
        out_shape=(jax.ShapeDtypeStruct((ch, px, py, nz), BF16),
                   jax.ShapeDtypeStruct((n_red * rows, 2 * cin), BF16)),
        in_specs=[hbm] * 4,
        out_specs=(vmem, vmem),
        scratch_shapes=[
            pltpu.VMEM((ch, px, py, nz), BF16),
            pltpu.VMEM((3, 9 * ch, cin), BF16),
            pltpu.VMEM((1, ch), F32),
            pltpu.VMEM((ch, px, py, nz), BF16),
            pltpu.VMEM((3, 9 * ch, cin), BF16),
            pltpu.VMEM((1, ch), F32),
            pltpu.VMEM((ch, px, py, nz), BF16),
            dma((4,)),
            pltpu.VMEM((px + 2, 2, ch, (py + 2) * nz), BF16),
            pltpu.VMEM((px + 2, cin, (py + 2) * nz), BF16),
            pltpu.VMEM((px, cin, inner), BF16),
            pltpu.VMEM((px, 3 * cin, inner), BF16),
            pltpu.VMEM((3, 3 * cin, 3 * cin), BF16),
            pltpu.VMEM((3, 3 * cin, 3 * cin), BF16),
            pltpu.VMEM((3, 3 * cin, 3 * cin), BF16),
            pltpu.VMEM((px, 2, ch, inner), F32),
            pltpu.VMEM((ch, px, py, nz), BF16),
            pltpu.VMEM((ch, px, py, nz), BF16),
            pltpu.VMEM((2 * n_red * rows, 2 * cin), BF16),
            pltpu.VMEM((n_turns, group * rows, 2 * cin), BF16),
            pltpu.VMEM((n_turns, rows, 2 * cin), BF16),
            pltpu.VMEM((n_red * rows, 2 * cin), BF16),
            dma((16,)), dma((16,)), dma((5,)), dma((5,)), dma((8,)), dma((8,)),
            dma((px,)), dma((px,)), dma, dma((n_turns,)), dma((n_turns,)), dma,
            pltpu.SemaphoreType.REGULAR((max(1, max(n_gx, n_gy) - 2),)),
        ],
        compiler_params=pltpu.CompilerParams(
            collective_id=0, has_side_effects=True, vmem_limit_bytes=24 * 1024 * 1024),
    )(*[pltpu.with_memory_space_constraint(v, pltpu.HBM) for v in (activations, filters.reshape(3, 9 * ch, cin), conv_bias.reshape(1, ch), grad_output)])
    input_grads, filter_grads, bias_grads = pl.pallas_call(
        functools.partial(unpack, (ch, cin)),
        out_shape=(jax.ShapeDtypeStruct(activations.shape, BF16),
                   jax.ShapeDtypeStruct((3, 9 * ch, cin), F32),
                   jax.ShapeDtypeStruct((1, ch), F32)),
        in_specs=[vmem] * 2,
        out_specs=(hbm,) * 3,
        scratch_shapes=[pltpu.VMEM((3, 9 * ch, cin), F32), pltpu.VMEM((1, ch), F32), dma((3,))],
        compiler_params=pltpu.CompilerParams(vmem_limit_bytes=8 * 1024 * 1024),
    )(igrad, packed)
    return (input_grads, filter_grads.reshape(filters.shape), bias_grads.reshape(ch))


def solution(mesh):
    return jax.shard_map(
        per_device,
        mesh=mesh,
        in_specs=(
            P("af", "gx", "gy", None),
            P(None, None, None, "af", None),
            P("af"),
            P("af", "gx", "gy", None),
        ),
        out_specs=(P("af", "gx", "gy", None), P(None, None, None, "af", None), P("af")),
        check_vma=False,
    )
```

```python
import functools
import math

import jax
import jax.numpy as jnp
from jax import lax
from jax.experimental import pallas as pl
from jax.experimental.pallas import tpu as pltpu
from jax.sharding import PartitionSpec as P

MESH = pl.DeviceIdType.MESH
F32, BF16 = jnp.float32, jnp.bfloat16
SIDES = [(dx, dy) for dx in (-1, 0, 1) for dy in (-1, 0, 1) if (dx, dy) != (0, 0)]
EARLY = [s for s, (dx, dy) in enumerate(SIDES) if dx <= 0]


def kernel(sizes, act_hbm, filt_hbm, bias_hbm, gout_hbm, igrad_ref, taps_ref, bias_out,
           act_ref, filt_ref, bias_ref, gout_ref, filt_in, bias_in, gout_in, load_sem, acts, gate, gout, gate_k, w_fwd, w_flip, w_bwd, part, ig_out, ig_in, pack, pack_in, mine, total,
           a_send, a_recv, c_send, c_recv, g_send, g_recv, q_send, q_recv, r_send, r_recv, t_send, t_recv, near):
    n_gx, n_gy, px, py, nz, ch, rows, n_red, factor = sizes
    cin = 2 * ch
    inner = py * nz
    gx, gy, af = lax.axis_index("gx"), lax.axis_index("gy"), lax.axis_index("af")
    other = 1 - af
    group = n_gx * n_gy
    me = gx * n_gy + gy
    rounds = max(1, max(n_gx, n_gy) - 2)
    core0, core1 = af == 0, af == 1

    def there(d):
        return (gx + d[0] >= 0) & (gx + d[0] < n_gx) & (gy + d[1] >= 0) & (gy + d[1] < n_gy)

    def back(d):
        return there((-d[0], -d[1]))

    barrier = pltpu.get_barrier_semaphore()
    around = sum(there(d).astype(jnp.int32) for d in SIDES)
    before = sum(there(SIDES[s]).astype(jnp.int32) for s in EARLY)

    def greet(d, core):
        pl.semaphore_signal(
            barrier, inc=1, device_id=(gx + d[0], gy + d[1], core), device_id_type=MESH)

    @pl.when(core1)
    def _():
        for d in SIDES:
            @pl.when(there(d))
            def _():
                greet(d, 1)
        for s in EARLY:
            @pl.when(back(SIDES[s]))
            def _():
                greet((-SIDES[s][0], -SIDES[s][1]), 0)

    pl.semaphore_signal(barrier, inc=1, device_id=(gx, gy, other), device_id_type=MESH)

    loads = [pltpu.make_async_copy(src, dst, load_sem.at[at]) for at, (src, dst) in enumerate((
        (act_hbm, act_ref), (filt_hbm, filt_ref), (bias_hbm, bias_ref), (gout_hbm, gout_ref)))]
    for load in loads:
        load.start()

    def tell(at):
        for d in SIDES:
            @pl.when(there(d))
            def _():
                pl.semaphore_signal(
                    near.at[at], inc=1, device_id=(gx + d[0], gy + d[1], 1), device_id_type=MESH)

    def hear(at):
        pl.semaphore_wait(near.at[at], around)

    def spans(d):
        dx, dy = d
        sx = {1: (px, 1), -1: (1, 1), 0: (1, px)}[dx]
        tx = {1: (0, 1), -1: (px + 1, 1), 0: (1, px)}[dx]
        sy = {1: (py, 1), -1: (1, 1), 0: (1, py)}[dy]
        ty = {1: (0, 1), -1: (py + 1, 1), 0: (1, py)}[dy]
        lanes = lambda s: pl.ds(s[0] * nz, s[1] * nz)
        return (pl.ds(*sx), lanes(sy)), (pl.ds(*tx), lanes(ty))

    for d in SIDES:
        tx, tl = spans(d)[1]

        @pl.when(~back(d) & core0)
        def _():
            gate[tx, :, tl] = jnp.zeros((tx.size, cin, tl.size), BF16)

        @pl.when(~back(d) & core1)
        def _():
            acts[tx, :, :, tl] = jnp.zeros((tx.size, 2, ch, tl.size), BF16)

    loads[0].wait()
    for xo in range(px):
        acts[xo + 1, pl.ds(af, 1), :, nz:nz + inner] = (
            act_ref[:, xo].reshape(1, ch, inner))
    pl.semaphore_wait(barrier, around * af + before * other + 1)

    def act_copy(s, half):
        d = SIDES[s]
        (sx, sl), (tx, tl) = spans(d)
        return pltpu.make_async_remote_copy(
            src_ref=acts.at[sx, half, :, sl], dst_ref=acts.at[tx, half, :, tl],
            send_sem=a_send.at[2 * s + half], recv_sem=a_recv.at[2 * s + half],
            device_id=(gx + d[0], gy + d[1], 1), device_id_type=MESH)

    def gate_copy(s):
        d = SIDES[s]
        (sx, sl), (tx, tl) = spans(d)
        return pltpu.make_async_remote_copy(
            src_ref=gate.at[sx, :, sl], dst_ref=gate.at[tx, :, tl],
            send_sem=g_send.at[s], recv_sem=g_recv.at[s],
            device_id=(gx + d[0], gy + d[1], 0), device_id_type=MESH)

    def across(at, src, dst):
        return pltpu.make_async_remote_copy(
            src_ref=src, dst_ref=dst, send_sem=c_send.at[at], recv_sem=c_recv.at[at],
            device_id=(gx, gy, other), device_id_type=MESH)

    block = acts.at[pl.ds(1, px), 0, :, pl.ds(nz, inner)]
    act_over = across(0, block, block)
    filt_over = across(1, filt_ref, filt_in)
    bias_over = across(2, bias_ref, bias_in)
    gout_over = across(3, gout_ref, gout_in)
    block = gate.at[pl.ds(1, px), :, pl.ds(nz, inner)]
    gate_over = across(4, block, block)

    def ig_over(xo):
        return pltpu.make_async_remote_copy(
            src_ref=ig_out.at[:, xo], dst_ref=ig_in.at[:, xo],
            send_sem=q_send.at[xo], recv_sem=q_recv.at[xo],
            device_id=(gx, gy, other), device_id_type=MESH)

    order = sorted(range(8), key=lambda s: (SIDES[s][0] == 0) * 2 + (SIDES[s][1] == 0))
    @pl.when(core0)
    def _():
        for s in order:
            if s in EARLY:
                @pl.when(there(SIDES[s]))
                def _():
                    act_copy(s, 0).start()
        act_over.start()

    @pl.when(core1)
    def _():
        for s in order:
            @pl.when(there(SIDES[s]))
            def _():
                act_copy(s, 1).start()
        act_over.wait_recv()
        for s in order:
            if s not in EARLY:
                @pl.when(there(SIDES[s]))
                def _():
                    act_copy(s, 0).start()
        tell(0)

    for load in loads[1:]:
        load.wait()
    filt_over.start()

    lane = lax.broadcasted_iota(jnp.int32, (1, nz), 1)

    def from_below(v):
        return jnp.where(lane == 0, 0.0, pltpu.roll(v, 1, 1))

    def from_above(v):
        return jnp.where(lane == nz - 1, 0.0, pltpu.roll(v, nz - 1, 1))

    step = 2 if py % 2 == 0 else 1
    head = ch
    main, fold = 3 * ch, 3 * ch // 2
    wide = lax.broadcasted_iota(jnp.int32, (1, 2 * cin), 1)

    def two_parts(v):
        high = v.astype(BF16).astype(F32)
        return jnp.where(wide < cin, high, v - high)

    def settle(ref, count, sem):
        block = ref.at[pl.ds(0, count * rows)]
        return pltpu.make_async_copy(block, block, sem)

    low = (n_gx - 1) // 2 * n_gy
    high = low + n_gy if n_gx > 1 else low
    pairs = n_gy // 2
    homes = [(low, high)[b % 2] + b // 2 % pairs * 2 for b in range(n_red)]
    turns = [b // 2 // pairs for b in range(n_red)]
    n_turns = turns[-1] + 1

    def scatter(first, count):
        for b in range(first, first + count):
            for h in (1, 0):
                chip = homes[b] + h
                block = pack.at[pl.ds((h * n_red + b) * rows, rows)]
                slot = pack_in.at[turns[b], pl.ds(pl.multiple_of(me * rows, 16), rows)]
                came = r_recv.at[turns[b]]

                @pl.when(me == chip)
                def _():
                    pltpu.make_async_copy(block, slot, came).start()

                @pl.when(me != chip)
                def _():
                    pltpu.make_async_remote_copy(
                        src_ref=block, dst_ref=slot, send_sem=r_send, recv_sem=came,
                        device_id=(chip // n_gy, chip % n_gy, 1), device_id_type=MESH).start()

    half = lax.rem(me, 2)
    at_block, has = [], []
    for turn in range(n_turns):
        at, found = jnp.int32(0), jnp.int32(0)
        for b in range(n_red):
            if turns[b] == turn:
                hit = (me - half == homes[b]).astype(jnp.int32)
                at, found = at + b * hit, found + hit
        at_block.append(pl.multiple_of(at * rows, 16))
        has.append(core1 & (found > 0))

    def give(turn, peer):
        pltpu.make_async_remote_copy(
            src_ref=mine.at[turn], dst_ref=total.at[pl.ds(at_block[turn], rows)],
            send_sem=t_send.at[turn], recv_sem=t_recv.at[turn],
            device_id=(peer // n_gy, peer % n_gy, half), device_id_type=MESH).start()

    def share(turn, peer):
        @pl.when(peer != me)
        def _():
            give(turn, peer)

    def keep(turn):
        @pl.when(half == 1)
        def _():
            pltpu.make_async_copy(mine.at[turn], total.at[pl.ds(at_block[turn], rows)], t_recv.at[turn]).start()

        @pl.when(half == 0)
        def _():
            give(turn, me)

    @pl.when(core1)
    def _():
        for i in range(3):
            for j in range(3):
                w_fwd[j, 3 * ch:6 * ch, i * cin:(i + 1) * cin] = filt_ref[i, j * 3 * ch:(j + 1) * 3 * ch, :]
        for xo in range(px):
            gout[xo, ch:2 * ch] = gout_ref[:, xo].reshape(ch, inner)
        filt_over.wait_recv()
        for i in range(3):
            for j in range(3):
                w_fwd[j, 0:3 * ch, i * cin:(i + 1) * cin] = filt_in[i, j * 3 * ch:(j + 1) * 3 * ch, :]
        bias_over.wait_recv()
        gout_over.wait_recv()
        for xo in range(px):
            gout[xo, 0:ch] = gout_in[:, xo].reshape(ch, inner)
        eye = (lax.broadcasted_iota(jnp.int32, (ch, ch), 0)
               == lax.broadcasted_iota(jnp.int32, (ch, ch), 1))
        bias = [jnp.sum(jnp.where(eye, ref[...], 0.0), axis=1, keepdims=True) for ref in (bias_in, bias_ref)]
        for at in range(1, rounds):
            hear(at - 1)
            tell(at)

        for s in reversed(order):
            @pl.when(back(SIDES[s]))
            def _():
                for h in range(2):
                    act_copy(s, h).wait_recv()

        sums = [jnp.zeros((ch, nz), F32)] * 2
        for xo in range(px):
            for y0 in range(0, py, step):
                acc = None
                for j in range(3):
                    window = acts[xo:xo + 3, :, :, (y0 + j) * nz:(y0 + j + step) * nz]
                    term = jnp.dot(w_fwd[j], window.reshape(3 * cin, step * nz),
                                   preferred_element_type=F32)
                    acc = term if acc is None else acc + term
                for h in range(2):
                    for u in range(step):
                        cut = acc[3 * h * ch:3 * (h + 1) * ch, u * nz:(u + 1) * nz]
                        pre = (cut[ch:2 * ch] + from_below(cut[:ch]) + from_above(cut[2 * ch:])) + bias[h]
                        lanes = slice((y0 + u) * nz, (y0 + u + 1) * nz)
                        squash = 1.0 / (1.0 + jnp.exp(-pre))
                        g = gout[xo, h * ch:(h + 1) * ch, lanes].astype(F32) * squash * (1.0 + pre * (1.0 - squash))
                        rounded = g.astype(BF16)
                        g = rounded.astype(F32)
                        sums[h] = sums[h] + g
                        gate[xo + 1, h * ch:(h + 1) * ch, (y0 + u + 1) * nz:(y0 + u + 2) * nz] = rounded
                        at = 3 * h * ch
                        gate_k[xo, at:at + ch, lanes] = from_above(g).astype(BF16)
                        gate_k[xo, at + ch:at + 2 * ch, lanes] = rounded
                        gate_k[xo, at + 2 * ch:at + 3 * ch, lanes] = from_below(g).astype(BF16)

        used = head + 3 * (main + fold)
        for h in range(2):
            first = h * n_red * rows
            whole = jnp.sum(sums[h], axis=1, keepdims=True) * factor + jnp.zeros((ch, 2 * cin), F32)
            pack[first:first + head, :] = two_parts(whole).astype(BF16)
            if n_red * rows > used:
                pack[first + used:first + n_red * rows, :] = jnp.zeros((n_red * rows - used, 2 * cin), BF16)

        ready = 0
        for j in range(3):
            both = None
            for xo in range(px):
                window = acts[xo:xo + 3, :, :, j * nz:j * nz + inner].reshape(3 * cin, inner)
                term = lax.dot_general(gate_k[xo], window, (((1,), (1,)), ((), ())),
                                       preferred_element_type=F32)
                both = term if both is None else both + term
            both = (both * factor).astype(BF16)
            for h in range(2):
                acc = both[3 * h * ch:3 * (h + 1) * ch]
                base = h * n_red * rows + head + j * (main + fold)
                pack[base:base + main, :] = acc[:, :2 * cin]
                pack[base + main:base + main + fold, 0:cin] = acc[:fold, 2 * cin:]
                pack[base + main:base + main + fold, cin:2 * cin] = acc[fold:, 2 * cin:]
            if j == 0:
                hear(rounds - 1)
            done = n_red if j == 2 else (head + (j + 1) * (main + fold)) // rows
            if done > ready:
                scatter(ready, done - ready)
            ready = done

        gate_over.start()
        for s in order:
            @pl.when(there(SIDES[s]))
            def _():
                gate_copy(s).start()

    @pl.when(core0)
    def _():
        bias_over.start()
        gout_over.start()
        filt_over.wait_recv()
        for i in range(3):
            for j in range(3):
                for k in range(3):
                    at = (3 * j + k) * ch
                    to = (2 - i) * cin
                    w_flip[j, to:to + ch, k * cin:(k + 1) * cin] = filt_ref[i, at:at + ch, :]
                    w_flip[j, to + ch:to + cin, k * cin:(k + 1) * cin] = filt_in[i, at:at + ch, :]
        for j in range(3):
            w_bwd[j] = w_flip[j].astype(F32).T.astype(BF16)

        gate_over.wait_recv()
        for s in order:
            @pl.when(back(SIDES[s]))
            def _():
                gate_copy(s).wait_recv()
        for xo in range(px):
            for y0 in range(0, py, step):
                acc = None
                for j in range(3):
                    at = y0 + 2 - j
                    window = gate[xo:xo + 3, :, at * nz:(at + step) * nz].reshape(3 * cin, step * nz)
                    term = jnp.dot(w_bwd[j], window, preferred_element_type=F32)
                    acc = term if acc is None else acc + term
                for u in range(step):
                    cut = acc[:, u * nz:(u + 1) * nz]
                    full = (cut[cin:2 * cin] + from_above(cut[:cin]) + from_below(cut[2 * cin:]))
                    part[xo, :, :, (y0 + u) * nz:(y0 + u + 1) * nz] = full.reshape(2, ch, nz)
            ig_out[:, xo] = part[xo, 1].reshape(ch, py, nz).astype(BF16)
            ig_over(xo).start()
            igrad_ref[:, xo] = part[xo, 0].reshape(ch, py, nz).astype(BF16)

    for turn in range(n_turns):
        @pl.when(has[turn])
        def _():
            settle(pack_in.at[turn], group, r_recv.at[turn]).wait()

            def add(t, v):
                return v + pack_in[turn, pl.ds(pl.multiple_of(t * rows, 16), rows), :].astype(F32)

            summed = pack_in[turn, 0:rows, :].astype(F32)
            if group <= 32:
                for t in range(1, group):
                    summed = add(t, summed)
            else:
                summed = lax.fori_loop(1, group, add, summed)
            both = two_parts(summed + pltpu.roll(summed, cin, 1))
            at = at_block[turn] + lax.broadcasted_iota(jnp.int32, (rows, 1), 0)
            mine[turn] = jnp.where(at < head, both, summed).astype(BF16)
            if group <= 32:
                for peer in sorted(range(group), key=lambda v: (v // n_gy, (0, 2, 1, 3)[v % n_gy] if n_gy == 4 else v)):
                    share(turn, peer)
            else:
                lax.fori_loop(0, group, lambda peer, _: share(turn, peer) or 0, 0)
            keep(turn)

    for s in order:
        @pl.when(there(SIDES[s]) & (core1 | (s in EARLY)))
        def _():
            act_copy(s, af).wait_send()

        @pl.when(there(SIDES[s]) & core1)
        def _():
            gate_copy(s).wait_send()
            if s not in EARLY:
                act_copy(s, 0).wait_send()
    filt_over.wait_send()

    @pl.when(core0)
    def _():
        act_over.wait_send()
        bias_over.wait_send()
        gout_over.wait_send()
        for xo in range(px):
            ig_over(xo).wait_send()

    @pl.when(core1)
    def _():
        gate_over.wait_send()
        for xo in range(px):
            ig_over(xo).wait_recv()
        igrad_ref[...] = ig_in[...]

    kept = sum(v.astype(jnp.int32) for v in has)
    for count in range(n_turns + 1):
        @pl.when(core1 & (kept == count))
        def _():
            settle(pack, 2 * n_red - count, r_send).wait()

    for turn in range(n_turns):
        @pl.when(has[turn] & (half == 1))
        def _():
            settle(pack_in.at[turn], group - 1, t_send.at[turn]).wait()

        @pl.when(has[turn] & (half == 0))
        def _():
            settle(pack_in.at[turn], group, t_send.at[turn]).wait()

    done = 0
    for turn in range(n_turns):
        settle(total, turns.count(turn), t_recv.at[turn]).wait()
        if turn == 0:
            lead = total[0:head, :].astype(F32)
            column = (lead + pltpu.roll(lead, cin, 1))[:, :1]
            eye = (lax.broadcasted_iota(jnp.int32, (ch, ch), 0)
                   == lax.broadcasted_iota(jnp.int32, (ch, ch), 1))
            bias_out[...] = jnp.sum(jnp.where(eye, column, 0.0), axis=0, keepdims=True)
        known = rows * sum(v <= turn for v in turns)
        while done < 3 and head + (done + 1) * (main + fold) <= known:
            base, at = head + done * (main + fold), done * main
            block = total[base:base + main + fold, :].astype(F32)
            taps_ref[0, at:at + main, :] = block[:main, :cin]
            taps_ref[1, at:at + main, :] = block[:main, cin:]
            taps_ref[2, at:at + fold, :] = block[main:, :cin]
            taps_ref[2, at + fold:at + main, :] = block[main:, cin:]
            done += 1


def write(*refs):
    copies = [pltpu.make_async_copy(refs[at], refs[3 + at], refs[6].at[at]) for at in range(3)]
    for copy in copies:
        copy.start()
    for copy in copies:
        copy.wait()


def per_device(activations, filters, conv_bias, grad_output):
    ch, px, py, nz = activations.shape
    n_gx, n_gy = lax.axis_size("gx"), lax.axis_size("gy")
    group = n_gx * n_gy
    cin = 2 * ch
    inner = py * nz
    factor = 1.0 / math.sqrt(px * n_gx * py * n_gy * nz)
    used = ch + 3 * (3 * ch + 3 * ch // 2)
    rows = 16 * (-(-(used // 16) // 6))
    n_red = -(-used // rows)
    n_turns = (n_red - 1) // 2 // (n_gy // 2) + 1

    vmem = pl.BlockSpec(memory_space=pltpu.VMEM)
    hbm = pl.BlockSpec(memory_space=pltpu.HBM)
    dma = pltpu.SemaphoreType.DMA
    parts = pl.pallas_call(
        functools.partial(kernel, (n_gx, n_gy, px, py, nz, ch, rows, n_red, factor)),
        out_shape=(jax.ShapeDtypeStruct((ch, px, py, nz), BF16),
                   jax.ShapeDtypeStruct((3, 9 * ch, cin), F32),
                   jax.ShapeDtypeStruct((1, ch), F32)),
        in_specs=[hbm] * 4,
        out_specs=(vmem,) * 3,
        scratch_shapes=[
            pltpu.VMEM((ch, px, py, nz), BF16),
            pltpu.VMEM((3, 9 * ch, cin), BF16),
            pltpu.VMEM((1, ch), F32),
            pltpu.VMEM((ch, px, py, nz), BF16),
            pltpu.VMEM((3, 9 * ch, cin), BF16),
            pltpu.VMEM((1, ch), F32),
            pltpu.VMEM((ch, px, py, nz), BF16),
            dma((4,)),
            pltpu.VMEM((px + 2, 2, ch, (py + 2) * nz), BF16),
            pltpu.VMEM((px + 2, cin, (py + 2) * nz), BF16),
            pltpu.VMEM((px, cin, inner), BF16),
            pltpu.VMEM((px, 3 * cin, inner), BF16),
            pltpu.VMEM((3, 3 * cin, 3 * cin), BF16),
            pltpu.VMEM((3, 3 * cin, 3 * cin), BF16),
            pltpu.VMEM((3, 3 * cin, 3 * cin), BF16),
            pltpu.VMEM((px, 2, ch, inner), F32),
            pltpu.VMEM((ch, px, py, nz), BF16),
            pltpu.VMEM((ch, px, py, nz), BF16),
            pltpu.VMEM((2 * n_red * rows, 2 * cin), BF16),
            pltpu.VMEM((n_turns, group * rows, 2 * cin), BF16),
            pltpu.VMEM((n_turns, rows, 2 * cin), BF16),
            pltpu.VMEM((n_red * rows, 2 * cin), BF16),
            dma((16,)), dma((16,)), dma((5,)), dma((5,)), dma((8,)), dma((8,)),
            dma((px,)), dma((px,)), dma, dma((n_turns,)), dma((n_turns,)), dma((n_turns,)),
            pltpu.SemaphoreType.REGULAR((max(1, max(n_gx, n_gy) - 2),)),
        ],
        compiler_params=pltpu.CompilerParams(
            collective_id=0, has_side_effects=True, vmem_limit_bytes=24 * 1024 * 1024),
    )(*[pltpu.with_memory_space_constraint(v, pltpu.HBM) for v in (activations, filters.reshape(3, 9 * ch, cin), conv_bias.reshape(1, ch), grad_output)])
    input_grads, filter_grads, bias_grads = pl.pallas_call(
        write,
        out_shape=(jax.ShapeDtypeStruct(activations.shape, BF16),
                   jax.ShapeDtypeStruct((3, 9 * ch, cin), F32),
                   jax.ShapeDtypeStruct((1, ch), F32)),
        in_specs=[vmem] * 3,
        out_specs=(hbm,) * 3,
        scratch_shapes=[dma((3,))],
        compiler_params=pltpu.CompilerParams(vmem_limit_bytes=8 * 1024 * 1024),
    )(*parts)
    return (input_grads, filter_grads.reshape(filters.shape), bias_grads.reshape(ch))


def solution(mesh):
    return jax.shard_map(
        per_device,
        mesh=mesh,
        in_specs=(
            P("af", "gx", "gy", None),
            P(None, None, None, "af", None),
            P("af"),
            P("af", "gx", "gy", None),
        ),
        out_specs=(P("af", "gx", "gy", None), P(None, None, None, "af", None), P("af")),
        check_vma=False,
    )
```

```python
import functools
import math

import jax
import jax.numpy as jnp
from jax import lax
from jax.experimental import pallas as pl
from jax.experimental.pallas import tpu as pltpu
from jax.sharding import PartitionSpec as P

MESH = pl.DeviceIdType.MESH
F32, BF16 = jnp.float32, jnp.bfloat16
SIDES = [(dx, dy) for dx in (-1, 0, 1) for dy in (-1, 0, 1) if (dx, dy) != (0, 0)]
EARLY = [s for s, (dx, dy) in enumerate(SIDES) if dx <= 0]


def kernel(sizes, act_hbm, filt_hbm, bias_hbm, gout_hbm, igrad_ref, taps_ref, bias_out,
           act_ref, filt_ref, bias_ref, gout_ref, filt_in, bias_in, gout_in, load_sem, acts, gate, gout, gate_k, w_fwd, w_flip, w_bwd, part, ig_out, ig_in, pack, pack_in, mine, total,
           a_send, a_recv, c_send, c_recv, g_send, g_recv, q_send, q_recv, r_send, r_recv, t_send, t_recv, near):
    n_gx, n_gy, px, py, nz, ch, rows, n_red, factor = sizes
    cin = 2 * ch
    inner = py * nz
    gx, gy, af = lax.axis_index("gx"), lax.axis_index("gy"), lax.axis_index("af")
    other = 1 - af
    group = n_gx * n_gy
    me = gx * n_gy + gy
    rounds = max(1, max(n_gx, n_gy) - 2)
    core0, core1 = af == 0, af == 1

    def there(d):
        return (gx + d[0] >= 0) & (gx + d[0] < n_gx) & (gy + d[1] >= 0) & (gy + d[1] < n_gy)

    def back(d):
        return there((-d[0], -d[1]))

    barrier = pltpu.get_barrier_semaphore()
    around = sum(there(d).astype(jnp.int32) for d in SIDES)
    before = sum(there(SIDES[s]).astype(jnp.int32) for s in EARLY)

    def greet(d, core):
        pl.semaphore_signal(
            barrier, inc=1, device_id=(gx + d[0], gy + d[1], core), device_id_type=MESH)

    @pl.when(core1)
    def _():
        for d in SIDES:
            @pl.when(there(d))
            def _():
                greet(d, 1)
        for s in EARLY:
            @pl.when(back(SIDES[s]))
            def _():
                greet((-SIDES[s][0], -SIDES[s][1]), 0)

    pl.semaphore_signal(barrier, inc=1, device_id=(gx, gy, other), device_id_type=MESH)

    loads = [pltpu.make_async_copy(src, dst, load_sem.at[at]) for at, (src, dst) in enumerate((
        (act_hbm, act_ref), (filt_hbm, filt_ref), (bias_hbm, bias_ref), (gout_hbm, gout_ref)))]
    for load in loads:
        load.start()

    def tell(at):
        for d in SIDES:
            @pl.when(there(d))
            def _():
                pl.semaphore_signal(
                    near.at[at], inc=1, device_id=(gx + d[0], gy + d[1], 1), device_id_type=MESH)

    def hear(at):
        pl.semaphore_wait(near.at[at], around)

    def spans(d):
        dx, dy = d
        sx = {1: (px, 1), -1: (1, 1), 0: (1, px)}[dx]
        tx = {1: (0, 1), -1: (px + 1, 1), 0: (1, px)}[dx]
        sy = {1: (py, 1), -1: (1, 1), 0: (1, py)}[dy]
        ty = {1: (0, 1), -1: (py + 1, 1), 0: (1, py)}[dy]
        lanes = lambda s: pl.ds(s[0] * nz, s[1] * nz)
        return (pl.ds(*sx), lanes(sy)), (pl.ds(*tx), lanes(ty))

    for d in SIDES:
        tx, tl = spans(d)[1]

        @pl.when(~back(d) & core0)
        def _():
            gate[tx, :, tl] = jnp.zeros((tx.size, cin, tl.size), BF16)

        @pl.when(~back(d) & core1)
        def _():
            acts[tx, :, :, tl] = jnp.zeros((tx.size, 2, ch, tl.size), BF16)

    loads[0].wait()
    for xo in range(px):
        acts[xo + 1, pl.ds(af, 1), :, nz:nz + inner] = (
            act_ref[:, xo].reshape(1, ch, inner))
    pl.semaphore_wait(barrier, around * af + before * other + 1)

    def act_copy(s, half):
        d = SIDES[s]
        (sx, sl), (tx, tl) = spans(d)
        return pltpu.make_async_remote_copy(
            src_ref=acts.at[sx, half, :, sl], dst_ref=acts.at[tx, half, :, tl],
            send_sem=a_send.at[2 * s + half], recv_sem=a_recv.at[2 * s + half],
            device_id=(gx + d[0], gy + d[1], 1), device_id_type=MESH)

    def gate_copy(s):
        d = SIDES[s]
        (sx, sl), (tx, tl) = spans(d)
        return pltpu.make_async_remote_copy(
            src_ref=gate.at[sx, :, sl], dst_ref=gate.at[tx, :, tl],
            send_sem=g_send.at[s], recv_sem=g_recv.at[s],
            device_id=(gx + d[0], gy + d[1], 0), device_id_type=MESH)

    def across(at, src, dst):
        return pltpu.make_async_remote_copy(
            src_ref=src, dst_ref=dst, send_sem=c_send.at[at], recv_sem=c_recv.at[at],
            device_id=(gx, gy, other), device_id_type=MESH)

    block = acts.at[pl.ds(1, px), 0, :, pl.ds(nz, inner)]
    act_over = across(0, block, block)
    filt_over = across(1, filt_ref, filt_in)
    bias_over = across(2, bias_ref, bias_in)
    gout_over = across(3, gout_ref, gout_in)
    block = gate.at[pl.ds(1, px), :, pl.ds(nz, inner)]
    gate_over = across(4, block, block)

    def ig_over(xo):
        return pltpu.make_async_remote_copy(
            src_ref=ig_out.at[:, xo], dst_ref=ig_in.at[:, xo],
            send_sem=q_send.at[xo], recv_sem=q_recv.at[xo],
            device_id=(gx, gy, other), device_id_type=MESH)

    order = sorted(range(8), key=lambda s: (SIDES[s][0] != 0 and SIDES[s][1] == 0, SIDES[s][0] == 0))
    @pl.when(core0)
    def _():
        for s in order:
            if s in EARLY:
                @pl.when(there(SIDES[s]))
                def _():
                    act_copy(s, 0).start()
        act_over.start()

    @pl.when(core1)
    def _():
        for s in order:
            @pl.when(there(SIDES[s]))
            def _():
                act_copy(s, 1).start()
        act_over.wait_recv()
        for s in order:
            if s not in EARLY:
                @pl.when(there(SIDES[s]))
                def _():
                    act_copy(s, 0).start()
        tell(0)

    for load in loads[1:]:
        load.wait()
    filt_over.start()

    lane = lax.broadcasted_iota(jnp.int32, (1, nz), 1)

    def from_below(v):
        return jnp.where(lane == 0, 0.0, pltpu.roll(v, 1, 1))

    def from_above(v):
        return jnp.where(lane == nz - 1, 0.0, pltpu.roll(v, nz - 1, 1))

    step = 2 if py % 2 == 0 else 1
    head = ch
    main, fold = 3 * ch, 3 * ch // 2
    wide = lax.broadcasted_iota(jnp.int32, (1, 2 * cin), 1)

    def two_parts(v):
        high = v.astype(BF16).astype(F32)
        return jnp.where(wide < cin, high, v - high)

    def settle(ref, count, sem):
        block = ref.at[pl.ds(0, count * rows)]
        return pltpu.make_async_copy(block, block, sem)

    low = (n_gx - 1) // 2 * n_gy
    high = low + n_gy if n_gx > 1 else low
    pairs = n_gy // 2
    homes = [(low, high)[b % 2] + b // 2 % pairs * 2 for b in range(n_red)]
    turns = [b // 2 // pairs for b in range(n_red)]
    n_turns = turns[-1] + 1

    def scatter(first, count):
        for b in range(first, first + count):
            for h in (1, 0):
                chip = homes[b] + h
                block = pack.at[pl.ds((h * n_red + b) * rows, rows)]
                slot = pack_in.at[turns[b], pl.ds(pl.multiple_of(me * rows, 16), rows)]
                came = r_recv.at[turns[b]]

                @pl.when(me == chip)
                def _():
                    pltpu.make_async_copy(block, slot, came).start()

                @pl.when(me != chip)
                def _():
                    pltpu.make_async_remote_copy(
                        src_ref=block, dst_ref=slot, send_sem=r_send, recv_sem=came,
                        device_id=(chip // n_gy, chip % n_gy, 1), device_id_type=MESH).start()

    half = lax.rem(me, 2)
    at_block, has = [], []
    for turn in range(n_turns):
        at, found = jnp.int32(0), jnp.int32(0)
        for b in range(n_red):
            if turns[b] == turn:
                hit = (me - half == homes[b]).astype(jnp.int32)
                at, found = at + b * hit, found + hit
        at_block.append(pl.multiple_of(at * rows, 16))
        has.append(core1 & (found > 0))

    def give(turn, peer):
        pltpu.make_async_remote_copy(
            src_ref=mine.at[turn], dst_ref=total.at[pl.ds(at_block[turn], rows)],
            send_sem=t_send.at[turn], recv_sem=t_recv.at[turn],
            device_id=(peer // n_gy, peer % n_gy, half), device_id_type=MESH).start()

    def share(turn, peer):
        @pl.when(peer != me)
        def _():
            give(turn, peer)

    def keep(turn):
        @pl.when(half == 1)
        def _():
            pltpu.make_async_copy(mine.at[turn], total.at[pl.ds(at_block[turn], rows)], t_recv.at[turn]).start()

        @pl.when(half == 0)
        def _():
            give(turn, me)

    @pl.when(core1)
    def _():
        for i in range(3):
            for j in range(3):
                w_fwd[j, 3 * ch:6 * ch, i * cin:(i + 1) * cin] = filt_ref[i, j * 3 * ch:(j + 1) * 3 * ch, :]
        for xo in range(px):
            gout[xo, ch:2 * ch] = gout_ref[:, xo].reshape(ch, inner)
        filt_over.wait_recv()
        for i in range(3):
            for j in range(3):
                w_fwd[j, 0:3 * ch, i * cin:(i + 1) * cin] = filt_in[i, j * 3 * ch:(j + 1) * 3 * ch, :]
        bias_over.wait_recv()
        gout_over.wait_recv()
        for xo in range(px):
            gout[xo, 0:ch] = gout_in[:, xo].reshape(ch, inner)
        eye = (lax.broadcasted_iota(jnp.int32, (ch, ch), 0)
               == lax.broadcasted_iota(jnp.int32, (ch, ch), 1))
        bias = [jnp.sum(jnp.where(eye, ref[...], 0.0), axis=1, keepdims=True) for ref in (bias_in, bias_ref)]
        for at in range(1, rounds):
            hear(at - 1)
            tell(at)

        for s in reversed(order):
            @pl.when(back(SIDES[s]))
            def _():
                for h in range(2):
                    act_copy(s, h).wait_recv()

        sums = [jnp.zeros((ch, nz), F32)] * 2
        for xo in range(px):
            for y0 in range(0, py, step):
                acc = None
                for j in range(3):
                    window = acts[xo:xo + 3, :, :, (y0 + j) * nz:(y0 + j + step) * nz]
                    term = jnp.dot(w_fwd[j], window.reshape(3 * cin, step * nz),
                                   preferred_element_type=F32)
                    acc = term if acc is None else acc + term
                for h in range(2):
                    for u in range(step):
                        cut = acc[3 * h * ch:3 * (h + 1) * ch, u * nz:(u + 1) * nz]
                        pre = (cut[ch:2 * ch] + from_below(cut[:ch]) + from_above(cut[2 * ch:])) + bias[h]
                        lanes = slice((y0 + u) * nz, (y0 + u + 1) * nz)
                        squash = 1.0 / (1.0 + jnp.exp(-pre))
                        g = gout[xo, h * ch:(h + 1) * ch, lanes].astype(F32) * squash * (1.0 + pre * (1.0 - squash))
                        rounded = g.astype(BF16)
                        g = rounded.astype(F32)
                        sums[h] = sums[h] + g
                        gate[xo + 1, h * ch:(h + 1) * ch, (y0 + u + 1) * nz:(y0 + u + 2) * nz] = rounded
                        at = 3 * h * ch
                        gate_k[xo, at:at + ch, lanes] = from_above(g).astype(BF16)
                        gate_k[xo, at + ch:at + 2 * ch, lanes] = rounded
                        gate_k[xo, at + 2 * ch:at + 3 * ch, lanes] = from_below(g).astype(BF16)

        used = head + 3 * (main + fold)
        for h in range(2):
            first = h * n_red * rows
            whole = jnp.sum(sums[h], axis=1, keepdims=True) * factor + jnp.zeros((ch, 2 * cin), F32)
            pack[first:first + head, :] = two_parts(whole).astype(BF16)
            if n_red * rows > used:
                pack[first + used:first + n_red * rows, :] = jnp.zeros((n_red * rows - used, 2 * cin), BF16)

        ready = 0
        for j in range(3):
            both = None
            for xo in range(px):
                window = acts[xo:xo + 3, :, :, j * nz:j * nz + inner].reshape(3 * cin, inner)
                term = lax.dot_general(gate_k[xo], window, (((1,), (1,)), ((), ())),
                                       preferred_element_type=F32)
                both = term if both is None else both + term
            both = (both * factor).astype(BF16)
            for h in range(2):
                acc = both[3 * h * ch:3 * (h + 1) * ch]
                base = h * n_red * rows + head + j * (main + fold)
                pack[base:base + main, :] = acc[:, :2 * cin]
                pack[base + main:base + main + fold, 0:cin] = acc[:fold, 2 * cin:]
                pack[base + main:base + main + fold, cin:2 * cin] = acc[fold:, 2 * cin:]
            if j == 0:
                hear(rounds - 1)
            done = n_red if j == 2 else (head + (j + 1) * (main + fold)) // rows
            if done > ready:
                scatter(ready, done - ready)
            ready = done

        gate_over.start()
        for s in order:
            @pl.when(there(SIDES[s]))
            def _():
                gate_copy(s).start()

    @pl.when(core0)
    def _():
        bias_over.start()
        gout_over.start()
        filt_over.wait_recv()
        for i in range(3):
            for j in range(3):
                for k in range(3):
                    at = (3 * j + k) * ch
                    to = (2 - i) * cin
                    w_flip[j, to:to + ch, k * cin:(k + 1) * cin] = filt_ref[i, at:at + ch, :]
                    w_flip[j, to + ch:to + cin, k * cin:(k + 1) * cin] = filt_in[i, at:at + ch, :]
        for j in range(3):
            w_bwd[j] = w_flip[j].astype(F32).T.astype(BF16)

        gate_over.wait_recv()
        for s in order:
            @pl.when(back(SIDES[s]))
            def _():
                gate_copy(s).wait_recv()
        for xo in range(px):
            for y0 in range(0, py, step):
                acc = None
                for j in range(3):
                    at = y0 + 2 - j
                    window = gate[xo:xo + 3, :, at * nz:(at + step) * nz].reshape(3 * cin, step * nz)
                    term = jnp.dot(w_bwd[j], window, preferred_element_type=F32)
                    acc = term if acc is None else acc + term
                for u in range(step):
                    cut = acc[:, u * nz:(u + 1) * nz]
                    full = (cut[cin:2 * cin] + from_above(cut[:cin]) + from_below(cut[2 * cin:]))
                    part[xo, :, :, (y0 + u) * nz:(y0 + u + 1) * nz] = full.reshape(2, ch, nz)
            ig_out[:, xo] = part[xo, 1].reshape(ch, py, nz).astype(BF16)
            ig_over(xo).start()
            igrad_ref[:, xo] = part[xo, 0].reshape(ch, py, nz).astype(BF16)

    for turn in range(n_turns):
        @pl.when(has[turn])
        def _():
            settle(pack_in.at[turn], group, r_recv.at[turn]).wait()

            def add(t, v):
                return v + pack_in[turn, pl.ds(pl.multiple_of(t * rows, 16), rows), :].astype(F32)

            summed = pack_in[turn, 0:rows, :].astype(F32)
            if group <= 32:
                for t in range(1, group):
                    summed = add(t, summed)
            else:
                summed = lax.fori_loop(1, group, add, summed)
            both = two_parts(summed + pltpu.roll(summed, cin, 1))
            at = at_block[turn] + lax.broadcasted_iota(jnp.int32, (rows, 1), 0)
            mine[turn] = jnp.where(at < head, both, summed).astype(BF16)
            if group <= 32:
                for peer in sorted(range(group), key=lambda v: (v // n_gy, (0, 2, 1, 3)[v % n_gy] if n_gy == 4 else v)):
                    share(turn, peer)
            else:
                lax.fori_loop(0, group, lambda peer, _: share(turn, peer) or 0, 0)
            keep(turn)

    for s in order:
        @pl.when(there(SIDES[s]) & (core1 | (s in EARLY)))
        def _():
            act_copy(s, af).wait_send()

        @pl.when(there(SIDES[s]) & core1)
        def _():
            gate_copy(s).wait_send()
            if s not in EARLY:
                act_copy(s, 0).wait_send()
    filt_over.wait_send()

    @pl.when(core0)
    def _():
        act_over.wait_send()
        bias_over.wait_send()
        gout_over.wait_send()
        for xo in range(px):
            ig_over(xo).wait_send()

    @pl.when(core1)
    def _():
        gate_over.wait_send()
        for xo in range(px):
            ig_over(xo).wait_recv()
        igrad_ref[...] = ig_in[...]

    kept = sum(v.astype(jnp.int32) for v in has)
    for count in range(n_turns + 1):
        @pl.when(core1 & (kept == count))
        def _():
            settle(pack, 2 * n_red - count, r_send).wait()

    for turn in range(n_turns):
        @pl.when(has[turn] & (half == 1))
        def _():
            settle(pack_in.at[turn], group - 1, t_send.at[turn]).wait()

        @pl.when(has[turn] & (half == 0))
        def _():
            settle(pack_in.at[turn], group, t_send.at[turn]).wait()

    done = 0
    for turn in range(n_turns):
        settle(total, turns.count(turn), t_recv.at[turn]).wait()
        if turn == 0:
            lead = total[0:head, :].astype(F32)
            column = (lead + pltpu.roll(lead, cin, 1))[:, :1]
            eye = (lax.broadcasted_iota(jnp.int32, (ch, ch), 0)
                   == lax.broadcasted_iota(jnp.int32, (ch, ch), 1))
            bias_out[...] = jnp.sum(jnp.where(eye, column, 0.0), axis=0, keepdims=True)
        known = rows * sum(v <= turn for v in turns)
        while done < 3 and head + (done + 1) * (main + fold) <= known:
            base, at = head + done * (main + fold), done * main
            block = total[base:base + main + fold, :].astype(F32)
            taps_ref[0, at:at + main, :] = block[:main, :cin]
            taps_ref[1, at:at + main, :] = block[:main, cin:]
            taps_ref[2, at:at + fold, :] = block[main:, :cin]
            taps_ref[2, at + fold:at + main, :] = block[main:, cin:]
            done += 1


def write(*refs):
    copies = [pltpu.make_async_copy(refs[at], refs[3 + at], refs[6].at[at]) for at in range(3)]
    for copy in copies:
        copy.start()
    for copy in copies:
        copy.wait()


def per_device(activations, filters, conv_bias, grad_output):
    ch, px, py, nz = activations.shape
    n_gx, n_gy = lax.axis_size("gx"), lax.axis_size("gy")
    group = n_gx * n_gy
    cin = 2 * ch
    inner = py * nz
    factor = 1.0 / math.sqrt(px * n_gx * py * n_gy * nz)
    used = ch + 3 * (3 * ch + 3 * ch // 2)
    rows = 16 * (-(-(used // 16) // 6))
    n_red = -(-used // rows)
    n_turns = (n_red - 1) // 2 // (n_gy // 2) + 1

    vmem = pl.BlockSpec(memory_space=pltpu.VMEM)
    hbm = pl.BlockSpec(memory_space=pltpu.HBM)
    dma = pltpu.SemaphoreType.DMA
    parts = pl.pallas_call(
        functools.partial(kernel, (n_gx, n_gy, px, py, nz, ch, rows, n_red, factor)),
        out_shape=(jax.ShapeDtypeStruct((ch, px, py, nz), BF16),
                   jax.ShapeDtypeStruct((3, 9 * ch, cin), F32),
                   jax.ShapeDtypeStruct((1, ch), F32)),
        in_specs=[hbm] * 4,
        out_specs=(vmem,) * 3,
        scratch_shapes=[
            pltpu.VMEM((ch, px, py, nz), BF16),
            pltpu.VMEM((3, 9 * ch, cin), BF16),
            pltpu.VMEM((1, ch), F32),
            pltpu.VMEM((ch, px, py, nz), BF16),
            pltpu.VMEM((3, 9 * ch, cin), BF16),
            pltpu.VMEM((1, ch), F32),
            pltpu.VMEM((ch, px, py, nz), BF16),
            dma((4,)),
            pltpu.VMEM((px + 2, 2, ch, (py + 2) * nz), BF16),
            pltpu.VMEM((px + 2, cin, (py + 2) * nz), BF16),
            pltpu.VMEM((px, cin, inner), BF16),
            pltpu.VMEM((px, 3 * cin, inner), BF16),
            pltpu.VMEM((3, 3 * cin, 3 * cin), BF16),
            pltpu.VMEM((3, 3 * cin, 3 * cin), BF16),
            pltpu.VMEM((3, 3 * cin, 3 * cin), BF16),
            pltpu.VMEM((px, 2, ch, inner), F32),
            pltpu.VMEM((ch, px, py, nz), BF16),
            pltpu.VMEM((ch, px, py, nz), BF16),
            pltpu.VMEM((2 * n_red * rows, 2 * cin), BF16),
            pltpu.VMEM((n_turns, group * rows, 2 * cin), BF16),
            pltpu.VMEM((n_turns, rows, 2 * cin), BF16),
            pltpu.VMEM((n_red * rows, 2 * cin), BF16),
            dma((16,)), dma((16,)), dma((5,)), dma((5,)), dma((8,)), dma((8,)),
            dma((px,)), dma((px,)), dma, dma((n_turns,)), dma((n_turns,)), dma((n_turns,)),
            pltpu.SemaphoreType.REGULAR((max(1, max(n_gx, n_gy) - 2),)),
        ],
        compiler_params=pltpu.CompilerParams(
            collective_id=0, has_side_effects=True, vmem_limit_bytes=24 * 1024 * 1024),
    )(*[pltpu.with_memory_space_constraint(v, pltpu.HBM) for v in (activations, filters.reshape(3, 9 * ch, cin), conv_bias.reshape(1, ch), grad_output)])
    input_grads, filter_grads, bias_grads = pl.pallas_call(
        write,
        out_shape=(jax.ShapeDtypeStruct(activations.shape, BF16),
                   jax.ShapeDtypeStruct((3, 9 * ch, cin), F32),
                   jax.ShapeDtypeStruct((1, ch), F32)),
        in_specs=[vmem] * 3,
        out_specs=(hbm,) * 3,
        scratch_shapes=[dma((3,))],
        compiler_params=pltpu.CompilerParams(vmem_limit_bytes=8 * 1024 * 1024),
    )(*parts)
    return (input_grads, filter_grads.reshape(filters.shape), bias_grads.reshape(ch))


def solution(mesh):
    return jax.shard_map(
        per_device,
        mesh=mesh,
        in_specs=(
            P("af", "gx", "gy", None),
            P(None, None, None, "af", None),
            P("af"),
            P("af", "gx", "gy", None),
        ),
        out_specs=(P("af", "gx", "gy", None), P(None, None, None, "af", None), P("af")),
        check_vma=False,
    )
```
